128 devices in a mesh: row: 16 (over x, z_lo, core), col: 8 (over z_hi, y).
Axes of the slice: x: 4, y: 4, z: 4 (z_hi: 2, z_lo: 2; z = z_hi * 2 + z_lo), core: 2. Of those that a mesh axis runs over, the one named last changes fastest.
Arguments:
- solution: float32 [524288, 64], P(('col', 'row')), may hold values from -6 to 6
- residual: float32 [98304, 64], P(('row', 'col')), may hold values from -6 to 6
- direction: float32 [524288, 64], P(('col', 'row')), may hold values from -6 to 6
- gradient: float32 [524288, 64], P(('col', 'row'))
- blocks: float32 [16, 2048, 128, 128], P('row', 'col'), may hold values from -0.078125 to 0.078125
- block_rows: int32 [16, 2048], P('row', 'col'), may hold values from 0 to 47
- block_cols: int32 [16, 2048], P('row', 'col'), may hold values from 0 to 511
- counts: int32 [16, 8], P('row', 'col'), may hold values from 64 to 256, as said below
Outputs:
- new_solution: float32 [524288, 64], P(('col', 'row'))
- new_residual: float32 [98304, 64], P(('row', 'col'))
- new_direction: float32 [524288, 64], P(('col', 'row'))
The draws below stay inside these ranges and needn't reach their ends.
Inputs may be any that keep to these rules, and one draw needn't show every extreme that they name: Some tile has all 256 slots live in every draw; the counts differ from tile to tile.
All inputs are finite; a program needn't handle non-finite values.
Results may differ from the reference program's by a relative error of at most 0.0001.
Values sent between devices are 32-bit elements; how exact they have to be, the bound alone decides.
No kernel may reach another device: no remote copies, remote signals or barrier semaphores. Data moves between devices by JAX's collectives and lax.ppermute only.
A program may use at most 192 MiB of HBM per device.

```python
import jax
import jax.numpy as jnp
from jax import lax

BS = 128
K = 64
CELLS = 524288
BR_TILE = 48
NB_DEV = 256
RAYS = 98304
N_ROW = 16
N_COL = 8


def draw_counts(key, part):
    key = jax.random.fold_in(key, 11)
    first_key, second_key = jax.random.split(key)
    lowest = max(1, NB_DEV // 4)
    values = jax.random.randint(first_key, (N_ROW, N_COL), lowest, NB_DEV + 1)
    chosen = jax.random.randint(second_key, (), 0, N_ROW * N_COL)
    flat_values = values.reshape(-1).at[chosen].set(NB_DEV)
    return flat_values.reshape(N_ROW, N_COL).astype(jnp.int32)


def draw_gradient(key, part):
    key = jax.random.fold_in(key, 23)
    first_key, second_key = jax.random.split(key)
    base_scale = 0.5 * (RAYS / CELLS) ** 0.5
    column_scale = jnp.exp(jax.random.uniform(second_key, (1, K), jnp.float32, -0.7, 0.7))
    values = jax.random.normal(first_key, (CELLS, K), jnp.float32)
    values = jnp.clip(values, -6.0, 6.0)
    return (values * column_scale * base_scale).astype(jnp.float32)


def place_ends(values, own_key, least, top_value):
    index_at = [jax.random.randint(jax.random.fold_in(own_key, axis), (), 0, length) for axis, length in enumerate(values.shape)]
    widest = values.shape.index(max(values.shape))
    beside = index_at[:widest] + [(index_at[widest] + 1) % values.shape[widest]] + index_at[widest + 1:]
    return values.at[tuple(index_at)].set(least).at[tuple(beside)].set(top_value)


def block_levels(key, extent, cuts, low, largest):
    def one(dim, parts):
        steps = jax.random.uniform(jax.random.fold_in(jax.random.fold_in(key, 6), dim), (parts,), jnp.float32, low / len(cuts), largest / len(cuts))
        return jnp.repeat(jnp.exp(steps), extent[dim] // parts).reshape((-1,) + (1,) * (len(extent) - dim - 1))

    loudness = one(*cuts[0])
    for cut in cuts[1:]:
        loudness = loudness * one(*cut)
    return loudness


def normal_values(stream_key, extent, scale, most, shards=(), kind=jnp.bfloat16):
    gain = block_levels(stream_key, extent, shards, -0.22, 0.18) if shards else 1.0
    result = jax.random.normal(stream_key, extent, jnp.float32) * scale * gain
    return jnp.minimum(jnp.maximum(result, -most), most).astype(kind)


def setup_inputs(seed: int = 0) -> dict:
    splits = jax.random.split(jax.random.key(seed), 9)
    solution = normal_values(splits[0], (CELLS, K), 1.0, 6.0, ((0, 128),), jnp.float32)
    residual = normal_values(splits[1], (RAYS, K), 1.0, 6.0, ((0, 128),), jnp.float32)
    direction = normal_values(splits[2], (CELLS, K), 1.0, 6.0, ((0, 128),), jnp.float32)
    gradient = draw_gradient(jax.random.fold_in(splits[8], 71), 0)
    blocks = normal_values(splits[4], (N_ROW, N_COL * NB_DEV, BS, BS), (BS * NB_DEV * N_COL // BR_TILE) ** -0.5, 0.078125, ((0, 16), (1, 8)), jnp.float32)
    block_rows = place_ends(jax.random.randint(splits[5], (N_ROW, N_COL * NB_DEV), 0, BR_TILE), jax.random.fold_in(splits[5], 1), 0, BR_TILE - 1).astype(jnp.int32)
    block_cols = place_ends(jax.random.randint(splits[6], (N_ROW, N_COL * NB_DEV), 0, CELLS // (N_COL * BS)), jax.random.fold_in(splits[6], 1), 0, (CELLS // (N_COL * BS)) - 1).astype(jnp.int32)
    counts = draw_counts(jax.random.fold_in(splits[8], 71), 0)
    return dict(solution=solution, residual=residual, direction=direction, gradient=gradient, blocks=blocks, block_rows=block_rows, block_cols=block_cols, counts=counts)


EPS = 1e-6


def tile_term(tile_blocks, gather_index, target_index, slot_live, source, target_count, transposed):
    picked = jnp.take(source, gather_index, axis=0)
    if transposed:
        product = jnp.einsum("bji,bjk->bik", tile_blocks, picked, precision=lax.Precision.HIGHEST)
    else:
        product = jnp.einsum("bij,bjk->bik", tile_blocks, picked, precision=lax.Precision.HIGHEST)
    product = product * slot_live[:, None, None]
    return jax.ops.segment_sum(product, target_index, num_segments=target_count)


def reference(solution, residual, direction, gradient, blocks, block_rows, block_cols, counts):
    cb_tile = CELLS // (N_COL * BS)
    tiles = blocks.reshape(N_ROW, N_COL, NB_DEV, BS, BS)
    rows_all = block_rows.reshape(N_ROW, N_COL, NB_DEV)
    cols_all = block_cols.reshape(N_ROW, N_COL, NB_DEV)
    live = (jnp.arange(NB_DEV, dtype=jnp.int32)[None, None, :] < counts[:, :, None]).astype(jnp.float32)
    panels = direction.reshape(N_COL, cb_tile, BS, K)
    gamma = jnp.sum(gradient * gradient, axis=0)

    def forward_row(row_index):
        accum = jnp.zeros((BR_TILE, BS, K), jnp.float32)
        for column in range(N_COL):
            accum = accum + tile_term(tiles[row_index, column], cols_all[row_index, column],
                                      rows_all[row_index, column], live[row_index, column],
                                      panels[column], BR_TILE, False)
        return accum

    image = lax.map(forward_row, jnp.arange(N_ROW, dtype=jnp.int32)).reshape(RAYS, K)
    alpha = gamma / (jnp.sum(image * image, axis=0) + EPS)
    new_solution = solution + alpha[None, :] * direction
    new_residual = residual - alpha[None, :] * image
    ray_tiles = new_residual.reshape(N_ROW, BR_TILE, BS, K)

    def backward_column(col_index):
        accum = jnp.zeros((cb_tile, BS, K), jnp.float32)
        for row_number in range(N_ROW):
            accum = accum + tile_term(tiles[row_number, col_index], rows_all[row_number, col_index],
                                      cols_all[row_number, col_index], live[row_number, col_index],
                                      ray_tiles[row_number], cb_tile, True)
        return accum

    new_gradient = lax.map(backward_column, jnp.arange(N_COL, dtype=jnp.int32)).reshape(CELLS, K)
    beta = jnp.sum(new_gradient * new_gradient, axis=0) / gamma
    new_direction = new_gradient + beta[None, :] * direction
    return new_solution, new_residual, new_direction
```

```python
import functools

import jax
import jax.numpy as jnp
from jax import lax
from jax.experimental import pallas as pl
from jax.experimental.pallas import tpu as pltpu
from jax.sharding import PartitionSpec as P

EPS = 1e-06
BS = 128
GROUP = 8
VMEM_BYTES = 56 * 1024 * 1024

NX, NZ, NCORE = 4, 2, 2
NZH, NY = 2, 4


def row_of(x, z, c):
    return (x % NX) * 4 + (z % NZ) * 2 + c % NCORE


def col_of(z, y):
    return (z % NZH) * 4 + y % NY


def row_shift(value, dx, dz, dc):
    pairs = [
        (row_of(x + dx, z + dz, c + dc), row_of(x, z, c))
        for x in range(NX)
        for z in range(NZ)
        for c in range(NCORE)
    ]
    return lax.ppermute(value, "row", pairs)


def col_shift(value, dz, dy):
    pairs = [(col_of(z + dz, y + dy), col_of(z, y)) for z in range(NZH) for y in range(NY)]
    return lax.ppermute(value, "col", pairs)


def sum_everywhere(row):
    count = NX * NZ * NCORE * NZH * NY
    sent = jnp.broadcast_to(row[None], (count, 1, row.shape[1]))
    got = lax.all_to_all(sent, ("row", "col"), 0, 0, tiled=True)
    return jnp.sum(got, axis=0)


def split(value):
    high = value.astype(jnp.bfloat16)
    low = (value - high.astype(jnp.float32)).astype(jnp.bfloat16)
    return high, low


def doubled(value):
    high, low = split(value)
    return jnp.concatenate(
        [jnp.concatenate([high, high], axis=1), jnp.concatenate([low, low], axis=1)], axis=0
    )


def forward_kernel(
    kc, places, rows_ref, cols_ref, meta_ref, blocks_ref, *refs
):
    pieces = refs[: len(places)]
    outs = refs[len(places) : len(places) + NY]
    panel, acc, sems = refs[len(places) + NY :]
    step = pl.program_id(0)
    count = meta_ref[0]
    x, z, c = meta_ref[1], meta_ref[2], meta_ref[3]
    half = kc // 2

    @pl.when(step == 0)
    def _():
        copies = []
        for number, (dx, dz, dc, stacked, part) in enumerate(places):
            for rel in range(NZ if stacked else 1):
                owner = ((x + dx) % NX) * 4 + ((z + dz + rel) % NZ) * 2 + (c + dc) % NCORE
                source = pieces[number].at[rel] if stacked else pieces[number]
                copies.append(
                    pltpu.make_async_copy(
                        source,
                        panel.at[owner, pl.ds(part * half, half), :],
                        sems.at[len(copies)],
                    )
                )
        for copy in copies:
            copy.start()
        acc[...] = jnp.zeros_like(acc)
        for copy in copies:
            copy.wait()

    base = step * GROUP

    def product(slot):
        cell = cols_ref[base + slot]
        offset = pl.multiple_of((cell % 32) * BS, BS)
        left = doubled(panel[cell // 32, :, pl.ds(offset, BS)])
        high, low = split(blocks_ref[slot])
        right = jnp.concatenate([high, low], axis=1)
        both = lax.dot_general(
            left, right, (((1,), (1,)), ((), ())), preferred_element_type=jnp.float32
        )
        live = jnp.where(base + slot < count, 1.0, 0.0)
        return (both[:kc] + both[kc:]) * live

    @pl.when(base < count)
    def _():
        terms = [product(slot) for slot in range(GROUP)]
        for slot in range(GROUP):
            acc[rows_ref[base + slot]] += terms[slot]

    @pl.when(step == pl.num_programs(0) - 1)
    def _():
        zh, y = meta_ref[4], meta_ref[5]
        per = acc.shape[0] // (NZH * NY)
        for dy in range(NY):
            for dz in range(NZH):
                piece = ((zh + dz) % NZH) * 4 + (y + dy) % NY
                for t in range(per):
                    outs[dy][dz, :, t * BS : (t + 1) * BS] = acc[piece * per + t]


def backward_kernel(
    kc, layout, rows_ref, cols_ref, meta_ref, blocks_ref, alpha_ref, *refs
):
    res = refs[:NY]
    img = refs[NY : 2 * NY]
    outs = refs[2 * NY : 2 * NY + len(layout)]
    source, acc, sems = refs[2 * NY + len(layout) :]
    step = pl.program_id(0)
    count = meta_ref[0]
    x, z, c = meta_ref[1], meta_ref[2], meta_ref[3]
    half = kc // 2

    @pl.when(step == 0)
    def _():
        zh, y = meta_ref[4], meta_ref[5]
        per = source.shape[0] // (NZH * NY)
        alpha = alpha_ref[...]
        for dy in range(NY):
            for dz in range(NZH):
                piece = ((zh + dz) % NZH) * 4 + (y + dy) % NY
                for t in range(per):
                    span = slice(t * BS, (t + 1) * BS)
                    value = res[dy][dz, :, span] - alpha * img[dy][dz, :, span]
                    source[piece * per + t] = doubled(value)

        def clear(i, _):
            acc[i] = jnp.zeros(acc.shape[1:], jnp.float32)
            return 0

        lax.fori_loop(0, acc.shape[0], clear, 0)

    base = step * GROUP

    def product(slot):
        left = source[rows_ref[base + slot]]
        high, low = split(blocks_ref[slot])
        right = jnp.concatenate([high, low], axis=0)
        both = lax.dot_general(
            left, right, (((1,), (0,)), ((), ())), preferred_element_type=jnp.float32
        )
        live = jnp.where(base + slot < count, 1.0, 0.0)
        return (both[:kc] + both[kc:]) * live

    @pl.when(base < count)
    def _():
        terms = [product(slot) for slot in range(GROUP)]
        for slot in range(GROUP):
            cell = cols_ref[base + slot]
            offset = pl.multiple_of((cell % 32) * BS, BS)
            acc[cell // 32, :, pl.ds(offset, BS)] += terms[slot]

    @pl.when(step == pl.num_programs(0) - 1)
    def _():
        copies = []
        for number, (part, dc, owners) in enumerate(layout):
            for rel, (dx, dz) in enumerate(owners):
                owner = ((x + dx) % NX) * 4 + ((z + dz) % NZ) * 2 + (c + dc) % NCORE
                target = outs[number].at[rel] if len(owners) > 1 else outs[number]
                copies.append(
                    pltpu.make_async_copy(
                        acc.at[owner, pl.ds(part * half, half), :],
                        target,
                        sems.at[len(copies)],
                    )
                )
        for copy in copies:
            copy.start()
        for copy in copies:
            copy.wait()


def block_map(step, rows_ref, cols_ref, meta_ref):
    last = jnp.maximum(meta_ref[0] - 1, 0) // GROUP
    return (jnp.minimum(step, last), 0, 0)


def fixed_map(rank):
    def index(step, rows_ref, cols_ref, meta_ref):
        return (0,) * rank

    return index


def cost(kc, slots):
    return pl.CostEstimate(
        flops=6 * slots * BS * BS * kc,
        bytes_accessed=4 * (slots * BS * BS + 2 * 16 * kc * 4096),
        transcendentals=0,
    )


def forward(blocks, rows, cols, meta, places, pieces, kc):
    slots = blocks.shape[0]
    any_spec = pl.BlockSpec(memory_space=pl.ANY)
    shape = (NZH, kc, 6 * BS)
    copies = sum(NZ if place[3] else 1 for place in places)
    return pl.pallas_call(
        functools.partial(forward_kernel, kc, places),
        grid_spec=pltpu.PrefetchScalarGridSpec(
            num_scalar_prefetch=3,
            grid=(slots // GROUP,),
            in_specs=[pl.BlockSpec((GROUP, BS, BS), block_map)] + [any_spec] * len(pieces),
            out_specs=[pl.BlockSpec(shape, fixed_map(3))] * NY,
            scratch_shapes=[
                pltpu.VMEM((16, kc, 4096), jnp.float32),
                pltpu.VMEM((48, kc, BS), jnp.float32),
                pltpu.SemaphoreType.DMA((copies,)),
            ],
        ),
        out_shape=[jax.ShapeDtypeStruct(shape, jnp.float32)] * NY,
        compiler_params=pltpu.CompilerParams(vmem_limit_bytes=VMEM_BYTES),
        cost_estimate=cost(kc, slots),
    )(rows, cols, meta, blocks, *pieces)


def backward(blocks, rows, cols, meta, alpha, res, img, layout, kc):
    slots = blocks.shape[0]
    any_spec = pl.BlockSpec(memory_space=pl.ANY)
    half = kc // 2
    tile = pl.BlockSpec(res[0].shape, fixed_map(3))
    shapes = [
        (half, 4096) if len(owners) == 1 else (len(owners), half, 4096)
        for _, _, owners in layout
    ]
    return pl.pallas_call(
        functools.partial(backward_kernel, kc, layout),
        grid_spec=pltpu.PrefetchScalarGridSpec(
            num_scalar_prefetch=3,
            grid=(slots // GROUP,),
            in_specs=[pl.BlockSpec((GROUP, BS, BS), block_map)]
            + [pl.BlockSpec((kc, 1), fixed_map(2))]
            + [tile] * (2 * NY),
            out_specs=[any_spec] * len(layout),
            scratch_shapes=[
                pltpu.VMEM((48, 2 * kc, 2 * BS), jnp.bfloat16),
                pltpu.VMEM((16, kc, 4096), jnp.float32),
                pltpu.SemaphoreType.DMA((sum(len(o) for _, _, o in layout),)),
            ],
        ),
        out_shape=[jax.ShapeDtypeStruct(shape, jnp.float32) for shape in shapes],
        compiler_params=pltpu.CompilerParams(vmem_limit_bytes=VMEM_BYTES),
        cost_estimate=cost(kc, slots),
    )(rows, cols, meta, blocks, alpha, *res, *img)


def gather_panel(chunk):
    half = chunk.shape[0] // 2
    first, second = chunk[:half], chunk[half:]
    places, pieces = [], []

    def add(value, dx, dz, stacked, part):
        places.append((dx, dz, 0, stacked, part))
        pieces.append(value)
        places.append((dx, dz, 1, stacked, part))
        pieces.append(row_shift(value, 0, 0, 1))

    first_z = row_shift(first, 0, 1, 0)
    second_x = {dx: row_shift(second, dx, 0, 0) for dx in (1, 3, 2)}
    pair = jnp.stack([first, first_z])
    first_x = {dx: row_shift(pair, dx, 0, 0) for dx in (1, 3, 2)}
    add(pair, 0, 0, True, 0)
    add(second, 0, 0, False, 1)
    add(row_shift(second, 0, 1, 0), 0, 1, False, 1)
    for dx in (1, 3, 2):
        add(second_x[dx], dx, 0, False, 1)
        add(row_shift(second_x[dx], 0, 1, 0), dx, 1, False, 1)
    for dx in (1, 3, 2):
        add(first_x[dx], dx, 0, True, 0)
    return tuple(places), pieces


def cell_layout():
    entries = []
    for dc in (1, 0):
        for dx in (2, 1, 3, 0):
            entries.append((1, dc, ((dx, 1),)))
        for dx in (1, 3, 2, 0):
            entries.append((0, dc, ((dx, 0), (dx, 1))))
        entries.append((1, dc, tuple((dx, 0) for dx in (2, 1, 3, 0))))
    return tuple(entries)


def scatter_cells(parts):
    other, own = parts[:9], parts[9:]
    summed = [mine + row_shift(sent, 0, 0, 1) for mine, sent in zip(own, other)]
    second_far = dict(zip((2, 1, 3, 0), summed[:4]))
    first = dict(zip((1, 3, 2, 0), summed[4:8]))
    second_near = dict(zip((2, 1, 3, 0), range(4)))
    second_got, first_got = [], []
    second_own = None
    for dx in (2, 1, 3, 0):
        term = summed[8][second_near[dx]] + row_shift(second_far[dx], 0, 1, 0)
        if dx:
            second_got.append(row_shift(term, -dx, 0, 0))
        else:
            second_own = term
    for dx in (1, 3, 2):
        first_got.append(row_shift(first[dx], -dx, 0, 0))
    pair = first[0] + first_got[0] + first_got[1] + first_got[2]
    first_own = pair[0] + row_shift(pair[1], 0, 1, 0)
    second_own = second_own + second_got[0] + second_got[1] + second_got[2]
    return jnp.concatenate([first_own, second_own], axis=0)


def per_device(solution, residual, direction, gradient, blocks, block_rows, block_cols, counts):
    tile_blocks = blocks[0]
    rows, cols = block_rows[0], block_cols[0]
    width = direction.shape[1]
    sol, res, dirn, grad = solution.T, residual.T, direction.T, gradient.T
    row_index, col_index = lax.axis_index("row"), lax.axis_index("col")
    meta = jnp.stack(
        [
            counts[0, 0],
            row_index // 4,
            (row_index // 2) % 2,
            row_index % 2,
            col_index // 4,
            col_index % 4,
        ]
    ).astype(jnp.int32)

    places, pieces = gather_panel(dirn)
    res_pair = jnp.stack([res, col_shift(res, 1, 0)])
    res_tile = [res_pair] + [col_shift(res_pair, 0, dy) for dy in (1, 2, 3)]

    image_parts = forward(tile_blocks, rows, cols, meta, places, pieces, width)
    got = [col_shift(image_parts[dy], 0, -dy) for dy in (1, 3, 2)]
    mine = image_parts[0] + got[0] + got[1] + got[2]
    image = mine[0] + col_shift(mine[1], 1, 0)
    image_pair = jnp.stack([image, col_shift(image, 1, 0)])
    image_tile = [image_pair] + [col_shift(image_pair, 0, dy) for dy in (1, 2, 3)]
    norms = jnp.concatenate([jnp.sum(grad * grad, axis=1), jnp.sum(image * image, axis=1)])
    norms = sum_everywhere(norms[None])[0]
    gamma, image_norms = norms[:width], norms[width:]
    alpha = (gamma / (image_norms + EPS))[:, None]

    layout = cell_layout()
    cell_parts = backward(
        tile_blocks, rows, cols, meta, alpha, res_tile, image_tile, layout, width
    )
    new_residual = res - alpha * image
    new_solution = sol + alpha * dirn
    new_gradient = scatter_cells(cell_parts)
    new_norms = jnp.sum(new_gradient * new_gradient, axis=1)
    new_norms = sum_everywhere(jnp.concatenate([new_norms, new_norms])[None])[0, :width]
    beta = (new_norms / gamma)[:, None]
    new_direction = new_gradient + beta * dirn
    return new_solution.T, new_residual.T, new_direction.T


def solution(mesh):
    placed = (
        P(("col", "row"), None),
        P(("row", "col"), None),
        P(("col", "row"), None),
        P(("col", "row"), None),
        P("row", "col", None, None),
        P("row", "col"),
        P("row", "col"),
        P("row", "col"),
    )
    return jax.shard_map(
        per_device,
        mesh=mesh,
        in_specs=placed,
        out_specs=(P(("col", "row"), None), P(("row", "col"), None), P(("col", "row"), None)),
        check_vma=False,
    )
```

```python
import functools

import jax
import jax.numpy as jnp
from jax import lax
from jax.experimental import pallas as pl
from jax.experimental.pallas import tpu as pltpu
from jax.sharding import PartitionSpec as P

EPS = 1e-06
BS = 128
GROUP = 16
HEAD = 8
CHUNKS = 1
VMEM_BYTES = 56 * 1024 * 1024

NX, NZ, NCORE = 4, 2, 2
NZH, NY = 2, 4


def row_of(x, z, c):
    return (x % NX) * 4 + (z % NZ) * 2 + c % NCORE


def col_of(z, y):
    return (z % NZH) * 4 + y % NY


def row_shift(value, dx, dz, dc):
    pairs = [
        (row_of(x + dx, z + dz, c + dc), row_of(x, z, c))
        for x in range(NX)
        for z in range(NZ)
        for c in range(NCORE)
    ]
    return lax.ppermute(value, "row", pairs)


def col_shift(value, dz, dy):
    pairs = [(col_of(z + dz, y + dy), col_of(z, y)) for z in range(NZH) for y in range(NY)]
    return lax.ppermute(value, "col", pairs)


def sum_over(row, axes):
    count = lax.axis_size(axes)
    sent = jnp.broadcast_to(row[None], (count, 1, row.shape[1]))
    return jnp.sum(lax.all_to_all(sent, axes, 0, 0, tiled=True), axis=0)


def split(value):
    high = value.astype(jnp.bfloat16)
    low = (value - high.astype(jnp.float32)).astype(jnp.bfloat16)
    return high, low


def doubled(value):
    high, low = split(value)
    return jnp.concatenate(
        [jnp.concatenate([high, high], axis=1), jnp.concatenate([low, low], axis=1)], axis=0
    )


def start_blocks(blocks, held, sems, groups):
    def start(group, _):
        span = pl.ds(group * GROUP, GROUP)
        pltpu.make_async_copy(blocks.at[span], held.at[span], sems.at[group]).start()
        return 0

    lax.fori_loop(0, groups, start, 0)


def wait_blocks(blocks, held, sems, group):
    span = pl.ds(group * GROUP, GROUP)
    pltpu.make_async_copy(blocks.at[span], held.at[span], sems.at[group]).wait()


def forward_kernel(kc, places, meta_ref, blocks_ref, *refs):
    pieces = refs[: len(places)]
    outs = refs[len(places) : len(places) + NY]
    panel, acc, held, sems, block_sems = refs[len(places) + NY :]
    count = meta_ref[0]
    x, z, c = meta_ref[1], meta_ref[2], meta_ref[3]
    groups = (count + GROUP - 1) // GROUP
    slots = held.shape[0]

    copies = []
    for number, (dc, entries) in enumerate(places):
        for first, size, (dx, dz), start in entries:
            owner = ((x + dx) % NX) * 4 + ((z + dz) % NZ) * 2 + (c + dc) % NCORE
            copies.append(
                pltpu.make_async_copy(
                    pieces[number].at[pl.ds(first, size)],
                    panel.at[owner, pl.ds(start, size), :],
                    sems.at[len(copies)],
                )
            )
    for copy in copies:
        copy.start()
    start_blocks(blocks_ref, held, block_sems, groups)
    acc[...] = jnp.zeros_like(acc)
    for copy in copies:
        copy.wait()

    def work(group, _):
        wait_blocks(blocks_ref, held, block_sems, group)
        for inner in range(GROUP):
            slot = group * GROUP + inner
            cell = meta_ref[HEAD + slots + slot]
            offset = pl.multiple_of((cell % 32) * BS, BS)
            left = doubled(panel[cell // 32, :, pl.ds(offset, BS)])
            high, low = split(held[slot])
            right = jnp.concatenate([high, low], axis=1)
            both = lax.dot_general(
                right, left, (((1,), (1,)), ((), ())), preferred_element_type=jnp.float32
            )
            live = jnp.where(slot < count, 1.0, 0.0)
            acc[meta_ref[HEAD + slot]] += both * live
        return 0

    lax.fori_loop(0, groups, work, 0)

    zh, y = meta_ref[4], meta_ref[5]
    per = acc.shape[0] // (NZH * NY)
    for dy in range(NY):
        for dz in range(NZH):
            piece = ((zh + dz) % NZH) * 4 + (y + dy) % NY
            for t in range(per):
                both = acc[piece * per + t].T
                outs[dy][dz, :, t * BS : (t + 1) * BS] = both[:kc] + both[kc:]


def backward_kernel(kc, layout, meta_ref, blocks_ref, alpha_ref, *refs):
    res = refs[:NY]
    img = refs[NY : 2 * NY]
    outs = refs[2 * NY : 2 * NY + len(layout)]
    source, acc, held, sems, block_sems = refs[2 * NY + len(layout) :]
    count = meta_ref[0]
    x, z, c = meta_ref[1], meta_ref[2], meta_ref[3]
    groups = (count + GROUP - 1) // GROUP
    slots = held.shape[0]
    start_blocks(blocks_ref, held, block_sems, groups)

    zh, y = meta_ref[4], meta_ref[5]
    per = source.shape[0] // (NZH * NY)
    alpha = alpha_ref[...]
    for dy in range(NY):
        for dz in range(NZH):
            piece = ((zh + dz) % NZH) * 4 + (y + dy) % NY
            for t in range(per):
                span = slice(t * BS, (t + 1) * BS)
                value = res[dy][dz, :, span] - alpha * img[dy][dz, :, span]
                source[piece * per + t] = doubled(value)

    def clear(i, _):
        acc[i] = jnp.zeros(acc.shape[1:], jnp.float32)
        return 0

    lax.fori_loop(0, acc.shape[0], clear, 0)

    def work(group, _):
        wait_blocks(blocks_ref, held, block_sems, group)
        for inner in range(GROUP):
            slot = group * GROUP + inner
            left = source[meta_ref[HEAD + slot]]
            high, low = split(held[slot])
            right = jnp.concatenate([high, low], axis=0)
            both = lax.dot_general(
                left, right, (((1,), (0,)), ((), ())), preferred_element_type=jnp.float32
            )
            live = jnp.where(slot < count, 1.0, 0.0)
            cell = meta_ref[HEAD + slots + slot]
            offset = pl.multiple_of((cell % 32) * BS, BS)
            acc[cell // 32, :, pl.ds(offset, BS)] += (both[:kc] + both[kc:]) * live
        return 0

    lax.fori_loop(0, groups, work, 0)

    copies = []
    for number, (dc, entries) in enumerate(layout):
        for first, size, (dx, dz), start in entries:
            owner = ((x + dx) % NX) * 4 + ((z + dz) % NZ) * 2 + (c + dc) % NCORE
            copies.append(
                pltpu.make_async_copy(
                    acc.at[owner, pl.ds(start, size), :],
                    outs[number].at[pl.ds(first, size)],
                    sems.at[len(copies)],
                )
            )
    for copy in copies:
        copy.start()
    for copy in copies:
        copy.wait()


def cost(kc, slots):
    return pl.CostEstimate(
        flops=6 * slots * BS * BS * kc,
        bytes_accessed=4 * (slots * BS * BS + 2 * 16 * kc * 4096),
        transcendentals=0,
    )


def forward(blocks, meta, places, pieces, kc):
    slots = blocks.shape[0]
    smem, vmem = pl.BlockSpec(memory_space=pltpu.SMEM), pl.BlockSpec(memory_space=pltpu.VMEM)
    any_spec = pl.BlockSpec(memory_space=pl.ANY)
    copies = sum(len(entries) for _, entries in places)
    return pl.pallas_call(
        functools.partial(forward_kernel, kc, places),
        in_specs=[smem] + [any_spec] * (1 + len(pieces)),
        out_specs=[vmem] * NY,
        scratch_shapes=[
            pltpu.VMEM((16, kc, 4096), jnp.float32),
            pltpu.VMEM((48, BS, 2 * kc), jnp.float32),
            pltpu.VMEM(blocks.shape, jnp.float32),
            pltpu.SemaphoreType.DMA((copies,)),
            pltpu.SemaphoreType.DMA((slots // GROUP,)),
        ],
        out_shape=[jax.ShapeDtypeStruct((NZH, kc, 6 * BS), jnp.float32)] * NY,
        compiler_params=pltpu.CompilerParams(vmem_limit_bytes=VMEM_BYTES),
        cost_estimate=cost(kc, slots),
    )(meta, blocks, *pieces)


def backward(blocks, meta, alpha, res, img, layout, kc):
    slots = blocks.shape[0]
    smem, vmem = pl.BlockSpec(memory_space=pltpu.SMEM), pl.BlockSpec(memory_space=pltpu.VMEM)
    any_spec = pl.BlockSpec(memory_space=pl.ANY)
    shapes = [(sum(entry[1] for entry in entries), 4096) for _, entries in layout]
    return pl.pallas_call(
        functools.partial(backward_kernel, kc, layout),
        in_specs=[smem] + [any_spec] + [vmem] * (1 + 2 * NY),
        out_specs=[any_spec] * len(layout),
        scratch_shapes=[
            pltpu.VMEM((48, 2 * kc, 2 * BS), jnp.bfloat16),
            pltpu.VMEM((16, kc, 4096), jnp.float32),
            pltpu.VMEM(blocks.shape, jnp.float32),
            pltpu.SemaphoreType.DMA((sum(len(entries) for _, entries in layout),)),
            pltpu.SemaphoreType.DMA((slots // GROUP,)),
        ],
        out_shape=[jax.ShapeDtypeStruct(shape, jnp.float32) for shape in shapes],
        compiler_params=pltpu.CompilerParams(vmem_limit_bytes=VMEM_BYTES),
        cost_estimate=cost(kc, slots),
    )(meta, blocks, alpha, *res, *img)


def after(*values):
    return lax.optimization_barrier(values)


def swap_core(value):
    return row_shift(value, 0, 0, 1)


def swap_z(value):
    return row_shift(value, 0, 1, 0)


def send_x(value, step):
    return row_shift(value, -step, 0, 0)


def shard_pieces(kc):
    h, q = kc // 2, kc // 4
    return (
        ((0, kc, (0, 0), 0),),
        ((0, kc, (0, 1), 0),),
        ((0, kc, (3, 0), 0),),
        ((0, kc, (1, 0), 0),),
        ((0, h, (3, 1), h), (h, h, (1, 1), h)),
        ((0, h, (2, 0), 0), (h, h, (3, 1), 0)),
        ((0, h, (2, 0), h), (h, h, (1, 1), 0)),
        ((0, h, (2, 1), h),),
        ((0, q, (2, 1), 0),),
        ((0, q, (2, 1), q),),
    )


def both_cores(kc):
    return tuple((dc, entries) for dc in range(NCORE) for entries in shard_pieces(kc))


def gather_panel(own):
    kc = own.shape[0]
    h, q = kc // 2, kc // 4
    z1, up1, down1 = swap_z(own), send_x(own, 1), send_x(own, -1)
    z1, up1, down1 = after(z1, up1, down1)
    z2 = swap_z(jnp.concatenate([up1[h:], down1[h:]]))
    up2 = send_x(jnp.concatenate([up1[:h], z1[:h]]), 1)
    down2 = send_x(jnp.concatenate([down1[h:], z1[:h]]), -1)
    z2, up2, down2 = after(z2, up2, down2)
    z3 = swap_z(down2[:h])
    up3, down3 = send_x(up2[h : h + q], 1), send_x(down2[h + q :], -1)
    pieces = [own, z1, up1, down1, z2, up2, down2, z3, up3, down3]
    return pieces + [swap_core(piece) for piece in pieces]


def scatter_cells(parts, kc):
    h, q = kc // 2, kc // 4
    count = len(parts) // 2
    terms = [mine + swap_core(sent) for mine, sent in zip(parts[:count], parts[count:])]
    own, z1, up1, down1, z2, up2, down2, z3, up3, down3 = terms
    z3, up3, down3 = swap_z(z3), send_x(up3, -1), send_x(down3, 1)
    z2, z3 = after(z2, z3)
    z2 = swap_z(z2)
    up2 = send_x(jnp.concatenate([up2[:h], up2[h : h + q] + up3, up2[h + q :]]), -1)
    down2 = send_x(jnp.concatenate([down2[:h] + z3, down2[h : h + q], down2[h + q :] + down3]), 1)
    z1 = swap_z(jnp.concatenate([z1[:h] + up2[h:] + down2[h:], z1[h:]]))
    up1 = send_x(up1 + jnp.concatenate([up2[:h], z2[:h]]), -1)
    down1 = send_x(down1 + jnp.concatenate([jnp.zeros_like(z2[:h]), down2[:h] + z2[h:]]), 1)
    return own + z1 + up1 + down1


def gather_rays(pair):
    return [pair] + [col_shift(pair, 0, dy) for dy in (1, 2, 3)]


def sum_rays(parts):
    got = [col_shift(parts[dy], 0, -dy) for dy in (1, 3, 2)]
    mine = parts[0] + got[0] + got[1] + got[2]
    return mine + col_shift(mine, 1, 0)[::-1]


def per_device(solution, residual, direction, gradient, blocks, block_rows, block_cols, counts):
    tile_blocks = blocks[0]
    width = direction.shape[1]
    kc = width // CHUNKS
    sol, res, dirn, grad = solution.T, residual.T, direction.T, gradient.T
    row_index, col_index = lax.axis_index("row"), lax.axis_index("col")
    head = [
        counts[0, 0],
        row_index // 4,
        (row_index // 2) % 2,
        row_index % 2,
        col_index // 4,
        col_index % 4,
    ]
    head = jnp.stack(head + [jnp.int32(0)] * (HEAD - len(head))).astype(jnp.int32)
    meta = jnp.concatenate([head, block_rows[0], block_cols[0]])
    layout = both_cores(kc)

    old_norms = jnp.sum(grad * grad, axis=1, keepdims=True)
    ride = jnp.concatenate([res, jnp.broadcast_to(old_norms, (width, BS))], axis=1)
    res_tile = gather_rays(jnp.stack([ride, col_shift(ride, 1, 0)]))
    old_norms = sum(jnp.sum(pair[:, :, -1], axis=0) for pair in res_tile)
    outputs = []
    for chunk in range(CHUNKS):
        span = slice(chunk * kc, (chunk + 1) * kc)
        s, r, d = sol[span], res[span], dirn[span]
        pieces = gather_panel(d)
        image_pair = sum_rays(forward(tile_blocks, meta, layout, pieces, kc))
        image = image_pair[0]
        image_tile = gather_rays(image_pair)
        norms = sum(jnp.sum(pair * pair, axis=(0, 2)) for pair in image_tile)
        norms = jnp.concatenate([old_norms[span], norms])
        norms = sum_over(jnp.pad(norms, (0, 128 - 2 * kc))[None], ("row",))[0]
        gamma, image_norms = norms[:kc], norms[kc : 2 * kc]
        alpha = (gamma / (image_norms + EPS))[:, None]
        cell_parts = backward(
            tile_blocks,
            meta,
            alpha,
            [pair[:, span] for pair in res_tile],
            image_tile,
            layout,
            kc,
        )
        new_gradient = scatter_cells(cell_parts, kc)
        new_norms = jnp.sum(new_gradient * new_gradient, axis=1)
        new_norms = jnp.pad(new_norms, (0, 128 - kc))[None]
        new_norms = sum_over(new_norms, ("row", "col"))[0, :kc]
        beta = (new_norms / gamma)[:, None]
        outputs.append((s + alpha * d, r - alpha * image, new_gradient + beta * d))
    return tuple(jnp.concatenate(parts, axis=0).T for parts in zip(*outputs))


def solution(mesh):
    placed = (
        P(("col", "row"), None),
        P(("row", "col"), None),
        P(("col", "row"), None),
        P(("col", "row"), None),
        P("row", "col", None, None),
        P("row", "col"),
        P("row", "col"),
        P("row", "col"),
    )
    return jax.shard_map(
        per_device,
        mesh=mesh,
        in_specs=placed,
        out_specs=(P(("col", "row"), None), P(("row", "col"), None), P(("col", "row"), None)),
        check_vma=False,
    )
```

```python
import functools

import jax
import jax.numpy as jnp
from jax import lax
from jax.experimental import pallas as pl
from jax.experimental.pallas import tpu as pltpu
from jax.sharding import PartitionSpec as P

EPS = 1e-06
BS = 128
GROUP = 16
HEAD = 8
YROWS = 40
VMEM_BYTES = 56 * 1024 * 1024

NX, NZ, NCORE = 4, 2, 2
NZH, NY = 2, 4


def row_of(x, z, c):
    return (x % NX) * 4 + (z % NZ) * 2 + c % NCORE


def col_of(z, y):
    return (z % NZH) * 4 + y % NY


def row_shift(value, dx, dz, dc):
    pairs = [
        (row_of(x + dx, z + dz, c + dc), row_of(x, z, c))
        for x in range(NX)
        for z in range(NZ)
        for c in range(NCORE)
    ]
    return lax.ppermute(value, "row", pairs)


def col_shift(value, dz, dy):
    pairs = [(col_of(z + dz, y + dy), col_of(z, y)) for z in range(NZH) for y in range(NY)]
    return lax.ppermute(value, "col", pairs)


def sum_over(row, axes):
    count = lax.axis_size(axes)
    sent = jnp.broadcast_to(row[None], (count, 1, row.shape[1]))
    return jnp.sum(lax.all_to_all(sent, axes, 0, 0, tiled=True), axis=0)


def split(value):
    high = value.astype(jnp.bfloat16)
    low = (value - high.astype(jnp.float32)).astype(jnp.bfloat16)
    return high, low


def doubled(value):
    high, low = split(value)
    return jnp.concatenate(
        [jnp.concatenate([high, high], axis=1), jnp.concatenate([low, low], axis=1)], axis=0
    )


def start_blocks(blocks, held, sems, groups):
    def start(group, _):
        span = pl.ds(group * GROUP, GROUP)
        pltpu.make_async_copy(blocks.at[span], held.at[span], sems.at[group]).start()
        return 0

    lax.fori_loop(0, groups, start, 0)


def wait_blocks(blocks, held, sems, group):
    span = pl.ds(group * GROUP, GROUP)
    pltpu.make_async_copy(blocks.at[span], held.at[span], sems.at[group]).wait()


def forward_kernel(kc, places, meta_ref, blocks_ref, *refs):
    pieces = refs[: len(places)]
    outs = refs[len(places) : len(places) + NY + NZH]
    panel, acc, held, sems, block_sems = refs[len(places) + NY + NZH :]
    count = meta_ref[0]
    x, z, c = meta_ref[1], meta_ref[2], meta_ref[3]
    groups = (count + GROUP - 1) // GROUP
    slots = held.shape[0]

    copies = []
    for number, (dc, entries) in enumerate(places):
        for first, size, (dx, dz), start in entries:
            owner = ((x + dx) % NX) * 4 + ((z + dz) % NZ) * 2 + (c + dc) % NCORE
            copies.append(
                pltpu.make_async_copy(
                    pieces[number].at[pl.ds(first, size)],
                    panel.at[owner, pl.ds(start, size), :],
                    sems.at[len(copies)],
                )
            )
    for copy in copies:
        copy.start()
    start_blocks(blocks_ref, held, block_sems, groups)
    acc[...] = jnp.zeros_like(acc)
    for copy in copies:
        copy.wait()

    def work(group, _):
        wait_blocks(blocks_ref, held, block_sems, group)
        for inner in range(GROUP):
            slot = group * GROUP + inner
            cell = meta_ref[HEAD + slots + slot]
            offset = pl.multiple_of((cell % 32) * BS, BS)
            left = doubled(panel[cell // 32, :, pl.ds(offset, BS)])
            high, low = split(held[slot])
            right = jnp.concatenate([high, low], axis=1)
            both = lax.dot_general(
                right, left, (((1,), (1,)), ((), ())), preferred_element_type=jnp.float32
            )
            live = jnp.where(slot < count, 1.0, 0.0)
            acc[meta_ref[HEAD + slot]] += both * live
        return 0

    lax.fori_loop(0, groups, work, 0)

    zh, y = meta_ref[4], meta_ref[5]
    per = acc.shape[0] // (NZH * NY)
    for dy in range(NY):
        for dz in range(NZH):
            piece = ((zh + dz) % NZH) * 4 + (y + dy) % NY
            for t in range(per):
                both = acc[piece * per + t].T
                both = both[:kc] + both[kc:]
                outs[dy][dz, :, t * BS : (t + 1) * BS] = both[:YROWS]
                outs[NY + dz][dy, :, t * BS : (t + 1) * BS] = both[YROWS:]


def backward_kernel(kc, layout, meta_ref, blocks_ref, alpha_ref, *refs):
    res = refs[:NY]
    img = refs[NY : 2 * NY]
    outs = refs[2 * NY : 2 * NY + len(layout)]
    source, acc, held, sems, block_sems = refs[2 * NY + len(layout) :]
    count = meta_ref[0]
    x, z, c = meta_ref[1], meta_ref[2], meta_ref[3]
    groups = (count + GROUP - 1) // GROUP
    slots = held.shape[0]
    start_blocks(blocks_ref, held, block_sems, groups)

    zh, y = meta_ref[4], meta_ref[5]
    per = source.shape[0] // (NZH * NY)
    alpha = alpha_ref[...]
    for dy in range(NY):
        for dz in range(NZH):
            piece = ((zh + dz) % NZH) * 4 + (y + dy) % NY
            for t in range(per):
                span = slice(t * BS, (t + 1) * BS)
                value = res[dy][dz, :, span] - alpha * img[dy][dz, :, span]
                source[piece * per + t] = doubled(value)

    def clear(i, _):
        acc[i] = jnp.zeros(acc.shape[1:], jnp.float32)
        return 0

    lax.fori_loop(0, acc.shape[0], clear, 0)

    def work(group, _):
        wait_blocks(blocks_ref, held, block_sems, group)
        for inner in range(GROUP):
            slot = group * GROUP + inner
            left = source[meta_ref[HEAD + slot]]
            high, low = split(held[slot])
            right = jnp.concatenate([high, low], axis=0)
            both = lax.dot_general(
                left, right, (((1,), (0,)), ((), ())), preferred_element_type=jnp.float32
            )
            live = jnp.where(slot < count, 1.0, 0.0)
            cell = meta_ref[HEAD + slots + slot]
            offset = pl.multiple_of((cell % 32) * BS, BS)
            acc[cell // 32, :, pl.ds(offset, BS)] += (both[:kc] + both[kc:]) * live
        return 0

    lax.fori_loop(0, groups, work, 0)

    copies = []
    for number, (dc, entries) in enumerate(layout):
        for first, size, (dx, dz), start in entries:
            owner = ((x + dx) % NX) * 4 + ((z + dz) % NZ) * 2 + (c + dc) % NCORE
            copies.append(
                pltpu.make_async_copy(
                    acc.at[owner, pl.ds(start, size), :],
                    outs[number].at[pl.ds(first, size)],
                    sems.at[len(copies)],
                )
            )
    for copy in copies:
        copy.start()
    for copy in copies:
        copy.wait()


def cost(kc, slots):
    return pl.CostEstimate(
        flops=6 * slots * BS * BS * kc,
        bytes_accessed=4 * (slots * BS * BS + 2 * 16 * kc * 4096),
        transcendentals=0,
    )


def forward(blocks, meta, places, pieces, kc):
    slots = blocks.shape[0]
    smem, vmem = pl.BlockSpec(memory_space=pltpu.SMEM), pl.BlockSpec(memory_space=pltpu.VMEM)
    any_spec = pl.BlockSpec(memory_space=pl.ANY)
    copies = sum(len(entries) for _, entries in places)
    return pl.pallas_call(
        functools.partial(forward_kernel, kc, places),
        in_specs=[smem] + [any_spec] * (1 + len(pieces)),
        out_specs=[vmem] * (NY + NZH),
        scratch_shapes=[
            pltpu.VMEM((16, kc, 4096), jnp.float32),
            pltpu.VMEM((48, BS, 2 * kc), jnp.float32),
            pltpu.VMEM(blocks.shape, jnp.float32),
            pltpu.SemaphoreType.DMA((copies,)),
            pltpu.SemaphoreType.DMA((slots // GROUP,)),
        ],
        out_shape=[jax.ShapeDtypeStruct((NZH, YROWS, 6 * BS), jnp.float32)] * NY
        + [jax.ShapeDtypeStruct((NY, kc - YROWS, 6 * BS), jnp.float32)] * NZH,
        compiler_params=pltpu.CompilerParams(vmem_limit_bytes=VMEM_BYTES),
        cost_estimate=cost(kc, slots),
    )(meta, blocks, *pieces)


def backward(blocks, meta, alpha, res, img, layout, kc):
    slots = blocks.shape[0]
    smem, vmem = pl.BlockSpec(memory_space=pltpu.SMEM), pl.BlockSpec(memory_space=pltpu.VMEM)
    any_spec = pl.BlockSpec(memory_space=pl.ANY)
    shapes = [(sum(entry[1] for entry in entries), 4096) for _, entries in layout]
    return pl.pallas_call(
        functools.partial(backward_kernel, kc, layout),
        in_specs=[smem] + [any_spec] + [vmem] * (1 + 2 * NY),
        out_specs=[any_spec] * len(layout),
        scratch_shapes=[
            pltpu.VMEM((48, 2 * kc, 2 * BS), jnp.bfloat16),
            pltpu.VMEM((16, kc, 4096), jnp.float32),
            pltpu.VMEM(blocks.shape, jnp.float32),
            pltpu.SemaphoreType.DMA((sum(len(entries) for _, entries in layout),)),
            pltpu.SemaphoreType.DMA((slots // GROUP,)),
        ],
        out_shape=[jax.ShapeDtypeStruct(shape, jnp.float32) for shape in shapes],
        compiler_params=pltpu.CompilerParams(vmem_limit_bytes=VMEM_BYTES),
        cost_estimate=cost(kc, slots),
    )(meta, blocks, alpha, *res, *img)


def after(*values):
    return lax.optimization_barrier(values)


def swap_core(value):
    return row_shift(value, 0, 0, 1)


def swap_z(value):
    return row_shift(value, 0, 1, 0)


def send_x(value, step):
    return row_shift(value, -step, 0, 0)


def shard_pieces(kc):
    h, q = kc // 2, kc // 4
    return (
        ((0, kc, (0, 0), 0),),
        ((0, kc, (0, 1), 0),),
        ((0, kc, (3, 0), 0),),
        ((0, kc, (1, 0), 0),),
        ((0, h, (3, 1), h), (h, h, (1, 1), h)),
        ((0, h, (2, 0), 0), (h, h, (3, 1), 0)),
        ((0, h, (2, 0), h), (h, h, (1, 1), 0)),
        ((0, h, (2, 1), h),),
        ((0, q, (2, 1), 0),),
        ((0, q, (2, 1), q),),
    )


def both_cores(kc):
    return tuple((dc, entries) for dc in range(NCORE) for entries in shard_pieces(kc))


def by_step(kc):
    pieces = shard_pieces(kc)
    layout = []
    for dc in range(NCORE):
        for step in (pieces[7:], pieces[4:7], pieces[:4]):
            entries, base = [], 0
            for piece in step:
                entries += [(base + first, size, owner, start) for first, size, owner, start in piece]
                base += sum(entry[1] for entry in piece)
            layout.append((dc, tuple(entries)))
    return tuple(layout)


def first_step(own):
    return swap_z(own), send_x(own, 1), send_x(own, -1)


def second_step(z1, up1, down1):
    h = z1.shape[0] // 2
    z2 = swap_z(jnp.concatenate([up1[h:], down1[h:]]))
    up2 = send_x(jnp.concatenate([up1[:h], z1[:h]]), 1)
    down2 = send_x(jnp.concatenate([down1[h:], z1[:h]]), -1)
    return z2, up2, down2


def third_step(z2, up2, down2):
    h = z2.shape[0] // 2
    q = h // 2
    return swap_z(down2[:h]), send_x(up2[h : h + q], 1), send_x(down2[h + q :], -1)


def with_core(pieces):
    return list(pieces) + [swap_core(piece) for piece in pieces]


def sum_cores(parts, kc):
    count = len(parts) // 2
    sent, got = list(parts[count:]), []
    for number in range(count):
        got.append(swap_core(sent[number]))
        if number + 1 < count:
            got[number], sent[number + 1] = after(got[number], sent[number + 1])
    steps = [mine + other for mine, other in zip(parts[:count], got)]
    pieces, sizes = [], [sum(entry[1] for entry in piece) for piece in shard_pieces(kc)]
    for step, numbers in zip(steps, ((7, 8, 9), (4, 5, 6), (0, 1, 2, 3))):
        base, cut = 0, []
        for number in numbers:
            cut.append(step[base : base + sizes[number]])
            base += sizes[number]
        pieces = cut + pieces
    return pieces


def third_back(z3, up3, down3):
    return swap_z(z3), send_x(up3, -1), send_x(down3, 1)


def second_back(z2, up2, down2, z3, up3, down3):
    h = z2.shape[0] // 2
    q = h // 2
    z2 = swap_z(z2)
    up2 = send_x(jnp.concatenate([up2[:h], up2[h : h + q] + up3, up2[h + q :]]), -1)
    down2 = send_x(jnp.concatenate([down2[:h] + z3, down2[h : h + q], down2[h + q :] + down3]), 1)
    return z2, up2, down2


def first_back(z1, up1, down1, z2, up2, down2):
    h = z2.shape[0] // 2
    z1 = swap_z(jnp.concatenate([z1[:h] + up2[h:] + down2[h:], z1[h:]]))
    up1 = send_x(up1 + jnp.concatenate([up2[:h], z2[:h]]), -1)
    down1 = send_x(jnp.concatenate([down1[:h], down1[h:] + down2[:h] + z2[h:]]), 1)
    return z1, up1, down1


def sum_rays(parts, far):
    first, near = parts[:NY], parts[NY] + far
    got = [col_shift(first[dy], 0, -dy) for dy in (1, 3, 2)]
    mine = first[0] + got[0] + got[1] + got[2]
    got = [col_shift(near[dy], 0, -dy) for dy in (1, 3, 2)]
    rest = near[0] + got[0] + got[1] + got[2]
    return mine[0] + col_shift(mine[1], 1, 0), rest


def spread_y(pair):
    return [pair] + [col_shift(pair, 0, dy) for dy in (1, 2, 3)]


def pad_row(row):
    return jnp.pad(row, (0, BS - row.shape[0]))[None]


def per_device(solution, residual, direction, gradient, blocks, block_rows, block_cols, counts):
    tile_blocks = blocks[0]
    width = direction.shape[1]
    kc = width
    sol, res, dirn, grad = solution.T, residual.T, direction.T, gradient.T
    row_index, col_index = lax.axis_index("row"), lax.axis_index("col")
    head = [
        counts[0, 0],
        row_index // 4,
        (row_index // 2) % 2,
        row_index % 2,
        col_index // 4,
        col_index % 4,
    ]
    head = jnp.stack(head + [jnp.int32(0)] * (HEAD - len(head))).astype(jnp.int32)
    meta = jnp.concatenate([head, block_rows[0], block_cols[0]])

    own = dirn
    first = first_step(own)
    first, meta = after(first, meta)
    own_other, z1_other = swap_core(own), swap_core(first[0])
    second = second_step(*first)
    ride, z1_other = after(res, z1_other)
    ride1, ride3 = col_shift(ride, 0, 1), col_shift(ride, 0, 3)
    second, ride1, ride3 = after(second, ride1, ride3)
    third = third_step(*second)
    others = [swap_core(piece) for piece in (*first[1:], *second)]
    ride, others = after(ride, others)
    ride2 = col_shift(ride, 0, 2)
    rides = jnp.stack([res, ride1, ride2, ride3])
    third, rides = after(third, rides)
    rides_z = col_shift(rides, 1, 0)
    others += [swap_core(piece) for piece in third]
    pieces = [own, *first, *second, *third, own_other, z1_other, *others]
    parts = forward(tile_blocks, meta, both_cores(kc), pieces, kc)

    far = col_shift(parts[NY + 1], 1, 0)
    far, rides_z = after(far, rides_z)
    rides = [jnp.stack([rides[dy], rides_z[dy]]) for dy in range(NY)]
    image = jnp.concatenate(sum_rays(parts, far))
    norms = jnp.concatenate([jnp.sum(grad * grad, axis=1), jnp.sum(image * image, axis=1)])
    pair = jnp.stack([image, col_shift(image, 1, 0)])
    norms, pair = after(norms, pair)
    image_tile = spread_y(pair)
    norms = sum_over(norms[None], ("row", "col"))[0]
    gamma = norms[:width]
    alpha = (gamma / (norms[width:] + EPS))[:, None]
    back = backward(tile_blocks, meta, alpha, rides, image_tile, by_step(kc), kc)
    own_back, z1, up1, down1, z2, up2, down2, z3, up3, down3 = sum_cores(back, kc)
    third = third_back(z3, up3, down3)
    z2, third = after(z2, third)
    second = second_back(z2, up2, down2, *third)
    z1, up1, down1 = first_back(z1, up1, down1, *second)
    new_gradient = own_back + z1 + up1 + down1
    new_norms = jnp.sum(new_gradient * new_gradient, axis=1)
    new_norms = sum_over(pad_row(new_norms), ("row", "col"))[0, :width]
    beta = (new_norms / gamma)[:, None]
    return (sol + alpha * dirn).T, (res - alpha * image).T, (new_gradient + beta * dirn).T


def solution(mesh):
    placed = (
        P(("col", "row"), None),
        P(("row", "col"), None),
        P(("col", "row"), None),
        P(("col", "row"), None),
        P("row", "col", None, None),
        P("row", "col"),
        P("row", "col"),
        P("row", "col"),
    )
    return jax.shard_map(
        per_device,
        mesh=mesh,
        in_specs=placed,
        out_specs=(P(("col", "row"), None), P(("row", "col"), None), P(("col", "row"), None)),
        check_vma=False,
    )
```

```python
import functools

import jax
import jax.numpy as jnp
from jax import lax
from jax.experimental import pallas as pl
from jax.experimental.pallas import tpu as pltpu
from jax.sharding import PartitionSpec as P

EPS = 1e-06
BS = 128
GROUP = 16
HEAD = 8
NEAR = ((0, 0), (0, 1), (3, 0), (1, 0), (2, 0), (3, 1), (1, 1))
SEQUENCE = tuple((dx, dz, dc) for dc in (0, 1) for dx, dz in NEAR) + ((2, 1, 0), (2, 1, 1))
YROWS = 40
BUFFERS = 6
VMEM_BYTES = 32 * 1024 * 1024

NX, NZ, NCORE = 4, 2, 2
NZH, NY = 2, 4


def row_of(x, z, c):
    return (x % NX) * 4 + (z % NZ) * 2 + c % NCORE


def col_of(z, y):
    return (z % NZH) * 4 + y % NY


def row_shift(value, dx, dz, dc):
    pairs = [
        (row_of(x + dx, z + dz, c + dc), row_of(x, z, c))
        for x in range(NX)
        for z in range(NZ)
        for c in range(NCORE)
    ]
    return lax.ppermute(value, "row", pairs)


def col_shift(value, dz, dy):
    pairs = [(col_of(z + dz, y + dy), col_of(z, y)) for z in range(NZH) for y in range(NY)]
    return lax.ppermute(value, "col", pairs)


def sum_over(row, axes):
    count = lax.axis_size(axes)
    sent = jnp.broadcast_to(row[None], (count, 1, row.shape[1]))
    return jnp.sum(lax.all_to_all(sent, axes, 0, 0, tiled=True), axis=0)


def split(value):
    high = value.astype(jnp.bfloat16)
    low = (value - high.astype(jnp.float32)).astype(jnp.bfloat16)
    return high, low


def doubled(value):
    high, low = split(value)
    return jnp.concatenate(
        [jnp.concatenate([high, high], axis=1), jnp.concatenate([low, low], axis=1)], axis=0
    )


def fetch(blocks, held, sems, meta_ref, group):
    buffer = group % BUFFERS
    for inner in range(GROUP):
        slot = meta_ref[HEAD + group * GROUP + inner]
        pltpu.make_async_copy(blocks.at[slot], held.at[buffer, inner], sems.at[buffer]).start()


def run_groups(blocks, held, sems, meta_ref, start, stop, total, work):
    def one(group, _):
        buffer = group % BUFFERS
        pltpu.make_async_copy(blocks.at[pl.ds(0, GROUP)], held.at[buffer], sems.at[buffer]).wait()
        work(group, buffer)

        @pl.when(group + BUFFERS < total)
        def _():
            fetch(blocks, held, sems, meta_ref, group + BUFFERS)

        return 0

    lax.fori_loop(start, stop, one, 0)


def fetch_first(blocks, held, sems, meta_ref, total):
    def one(group, _):
        fetch(blocks, held, sems, meta_ref, group)
        return 0

    lax.fori_loop(0, jnp.minimum(total, BUFFERS), one, 0)


def ends_of(meta_ref, slots, position):
    return meta_ref[HEAD + 3 * (slots + GROUP) + position]


def owner_of(meta_ref, place):
    dx, dz, dc = place
    x, z, c = meta_ref[1], meta_ref[2], meta_ref[3]
    return ((x + dx) % NX) * 4 + ((z + dz) % NZ) * 2 + (c + dc) % NCORE


def forward_kernel(kc, slots, stages, places, meta_ref, blocks_ref, *refs):
    pieces = refs[: len(places)]
    outs = refs[len(places) : len(places) + NY + NZH]
    acc, panel, held, sems, block_sems = refs[len(places) + NY + NZH :]
    last = ends_of(meta_ref, slots, len(SEQUENCE) - 1)
    total = (last + GROUP - 1) // GROUP

    copies = []
    for number, (dc, entries) in enumerate(places):
        for source, size, (dx, dz), start in entries:
            position = SEQUENCE.index((dx, dz, dc))
            copy = pltpu.make_async_copy(
                pieces[number].at[pl.ds(source, size)],
                panel.at[position, pl.ds(start, size), :],
                sems.at[len(copies)],
            )
            copies.append((position, copy))
    for _, copy in copies:
        copy.start()
    fetch_first(blocks_ref, held, block_sems, meta_ref, total)
    acc[...] = jnp.zeros_like(acc)

    def work(group, buffer):
        for inner in range(GROUP):
            slot = group * GROUP + inner
            place = meta_ref[HEAD + 2 * (slots + GROUP) + slot]
            offset = pl.multiple_of((place % 32) * BS, BS)
            left = doubled(panel[place // 32, :, pl.ds(offset, BS)])
            high, low = split(held[buffer, inner])
            right = jnp.concatenate([high, low], axis=1)
            both = lax.dot_general(
                right, left, (((1,), (1,)), ((), ())), preferred_element_type=jnp.float32
            )
            live = jnp.where(slot < last, 1.0, 0.0)
            acc[meta_ref[HEAD + slots + GROUP + slot]] += both * live

    done, waited = 0, 0
    for stage in stages:
        for position, copy in copies:
            if waited <= position < stage:
                copy.wait()
        waited = stage
        stop = total if stage == stages[-1] else ends_of(meta_ref, slots, stage - 1) // GROUP
        run_groups(blocks_ref, held, block_sems, meta_ref, done, stop, total, work)
        done = stop

    zh, y = meta_ref[4], meta_ref[5]
    per = acc.shape[0] // (NZH * NY)
    for dy in range(NY):
        for dz in range(NZH):
            piece = ((zh + dz) % NZH) * 4 + (y + dy) % NY
            for t in range(per):
                both = acc[piece * per + t].T
                both = both[:kc] + both[kc:]
                outs[dy][dz, :, t * BS : (t + 1) * BS] = both[:YROWS]
                outs[NY + dz][dy, :, t * BS : (t + 1) * BS] = both[YROWS:]


def backward_kernel(kc, slots, stages, layout, meta_ref, blocks_ref, alpha_ref, *refs):
    res = refs[:NY]
    img = refs[NY : 2 * NY]
    outs = refs[2 * NY : 2 * NY + len(layout)]
    source, acc, held, sems, block_sems = refs[2 * NY + len(layout) :]
    last = ends_of(meta_ref, slots, len(SEQUENCE) - 1)
    total = (last + GROUP - 1) // GROUP
    fetch_first(blocks_ref, held, block_sems, meta_ref, total)

    zh, y = meta_ref[4], meta_ref[5]
    per = source.shape[0] // (NZH * NY)
    alpha = alpha_ref[...]
    for dy in range(NY):
        for dz in range(NZH):
            piece = ((zh + dz) % NZH) * 4 + (y + dy) % NY
            for t in range(per):
                span = slice(t * BS, (t + 1) * BS)
                value = res[dy][dz, :, span] - alpha * img[dy][dz, :, span]
                source[piece * per + t] = doubled(value)

    def clear(i, _):
        acc[i] = jnp.zeros(acc.shape[1:], jnp.float32)
        return 0

    lax.fori_loop(0, acc.shape[0], clear, 0)

    def work(group, buffer):
        for inner in range(GROUP):
            slot = group * GROUP + inner
            left = source[meta_ref[HEAD + slots + GROUP + slot]]
            high, low = split(held[buffer, inner])
            right = jnp.concatenate([high, low], axis=0)
            both = lax.dot_general(
                left, right, (((1,), (0,)), ((), ())), preferred_element_type=jnp.float32
            )
            live = jnp.where(slot < last, 1.0, 0.0)
            place = meta_ref[HEAD + 2 * (slots + GROUP) + slot]
            offset = pl.multiple_of((place % 32) * BS, BS)
            acc[place // 32, :, pl.ds(offset, BS)] += (both[:kc] + both[kc:]) * live

    copies = []
    for number, (dc, entries) in enumerate(layout):
        for target, size, (dx, dz), start in entries:
            position = SEQUENCE.index((dx, dz, dc))
            copy = pltpu.make_async_copy(
                acc.at[position, pl.ds(start, size), :],
                outs[number].at[pl.ds(target, size)],
                sems.at[len(copies)],
            )
            copies.append((position, copy))
    done, sent = 0, 0
    for stage in stages:
        stop = (ends_of(meta_ref, slots, stage - 1) + GROUP - 1) // GROUP
        run_groups(blocks_ref, held, block_sems, meta_ref, done, stop, total, work)
        done = stop
        for position, copy in copies:
            if sent <= position < stage:
                copy.start()
        sent = stage
    for _, copy in copies:
        copy.wait()


def cost(kc, slots, shards):
    return pl.CostEstimate(
        flops=6 * slots * BS * BS * kc,
        bytes_accessed=4 * (slots * BS * BS + 2 * shards * kc * 4096),
        transcendentals=0,
    )


def forward(blocks, meta, places, pieces, kc, stages):
    slots = blocks.shape[0]
    smem, vmem = pl.BlockSpec(memory_space=pltpu.SMEM), pl.BlockSpec(memory_space=pltpu.VMEM)
    any_spec = pl.BlockSpec(memory_space=pl.ANY)
    out_shape = [jax.ShapeDtypeStruct((NZH, YROWS, 6 * BS), jnp.float32)] * NY
    out_shape += [jax.ShapeDtypeStruct((NY, kc - YROWS, 6 * BS), jnp.float32)] * NZH
    return pl.pallas_call(
        functools.partial(forward_kernel, kc, slots, stages, places),
        in_specs=[smem] + [any_spec] * (1 + len(pieces)),
        out_specs=[vmem] * len(out_shape),
        scratch_shapes=[
            pltpu.VMEM((48, BS, 2 * kc), jnp.float32),
            pltpu.VMEM((16, kc, 4096), jnp.float32),
            pltpu.VMEM((BUFFERS, GROUP, BS, BS), jnp.float32),
            pltpu.SemaphoreType.DMA((sum(len(entries) for _, entries in places),)),
            pltpu.SemaphoreType.DMA((BUFFERS,)),
        ],
        out_shape=out_shape,
        compiler_params=pltpu.CompilerParams(vmem_limit_bytes=VMEM_BYTES),
        cost_estimate=cost(kc, slots, len(SEQUENCE)),
    )(meta, blocks, *pieces)


def backward(blocks, meta, alpha, res, img, layout, kc, stages):
    slots = blocks.shape[0]
    smem, vmem = pl.BlockSpec(memory_space=pltpu.SMEM), pl.BlockSpec(memory_space=pltpu.VMEM)
    any_spec = pl.BlockSpec(memory_space=pl.ANY)
    shapes = [(sum(entry[1] for entry in entries), 4096) for _, entries in layout]
    return pl.pallas_call(
        functools.partial(backward_kernel, kc, slots, stages, layout),
        in_specs=[smem] + [any_spec] + [vmem] * (1 + 2 * NY),
        out_specs=[any_spec] * len(layout),
        scratch_shapes=[
            pltpu.VMEM((48, 2 * kc, 2 * BS), jnp.bfloat16),
            pltpu.VMEM((16, kc, 4096), jnp.float32),
            pltpu.VMEM((BUFFERS, GROUP, BS, BS), jnp.float32),
            pltpu.SemaphoreType.DMA((sum(len(entries) for _, entries in layout),)),
            pltpu.SemaphoreType.DMA((BUFFERS,)),
        ],
        out_shape=[jax.ShapeDtypeStruct(shape, jnp.float32) for shape in shapes],
        compiler_params=pltpu.CompilerParams(vmem_limit_bytes=VMEM_BYTES),
        cost_estimate=cost(kc, slots, len(SEQUENCE)),
    )(meta, blocks, alpha, *res, *img)


def sorted_slots(rows, cols, count, x, z, c):
    slots = rows.shape[0]
    number = jnp.arange(slots, dtype=jnp.int32)
    owner = cols // 32
    code = ((owner // 4 - x) % NX) * 4 + ((owner // 2 - z) % NZ) * 2 + (owner - c) % NCORE
    codes = jnp.array([dx * 4 + dz * 2 + dc for dx, dz, dc in SEQUENCE], jnp.int32)
    steps = jnp.arange(len(SEQUENCE), dtype=jnp.int32)
    position = jnp.sum(jnp.where(code[:, None] == codes, steps, 0), axis=1)
    live = number < count
    key = jnp.where(live, position, len(SEQUENCE)) * slots + number
    rank = jnp.sum((key[None] < key[:, None]).astype(jnp.int32), axis=1)
    where = rank[None] == number[:, None]
    place = position * 32 + cols % 32
    lists = [jnp.sum(jnp.where(where, value[None], 0), axis=1) for value in (number, rows, place)]
    ends = jnp.sum((live[None] & (position[None] <= steps[:, None])).astype(jnp.int32), axis=1)
    pad = jnp.zeros((GROUP,), jnp.int32)
    return jnp.concatenate([part for value in lists for part in (value, pad)] + [ends])


def after(*values):
    return lax.optimization_barrier(values)


def swap_core(value):
    return row_shift(value, 0, 0, 1)


def swap_z(value):
    return row_shift(value, 0, 1, 0)


def send_x(value, step):
    return row_shift(value, -step, 0, 0)


def shard_pieces(kc):
    h, q = kc // 2, kc // 4
    return (
        ((0, kc, (0, 0), 0),),
        ((0, kc, (0, 1), 0),),
        ((0, kc, (3, 0), 0),),
        ((0, kc, (1, 0), 0),),
        ((0, h, (3, 1), h), (h, h, (1, 1), h)),
        ((0, h, (2, 0), 0), (h, h, (3, 1), 0)),
        ((0, h, (2, 0), h), (h, h, (1, 1), 0)),
        ((0, h, (2, 1), h),),
        ((0, q, (2, 1), 0),),
        ((0, q, (2, 1), q),),
    )


def both_cores(kc):
    return tuple((dc, entries) for dc in range(NCORE) for entries in shard_pieces(kc))


def by_step(kc):
    pieces = shard_pieces(kc)
    layout = []
    for dc in range(NCORE):
        for step in (pieces[7:], pieces[4:7], pieces[:4]):
            entries, base = [], 0
            for piece in step:
                entries += [(base + first, size, owner, start) for first, size, owner, start in piece]
                base += sum(entry[1] for entry in piece)
            layout.append((dc, tuple(entries)))
    return tuple(layout)


def first_step(own):
    return swap_z(own), send_x(own, 1), send_x(own, -1)


def second_step(z1, up1, down1):
    h = z1.shape[0] // 2
    z2 = swap_z(jnp.concatenate([up1[h:], down1[h:]]))
    up2 = send_x(jnp.concatenate([up1[:h], z1[:h]]), 1)
    down2 = send_x(jnp.concatenate([down1[h:], z1[:h]]), -1)
    return z2, up2, down2


def third_step(z2, up2, down2):
    h = z2.shape[0] // 2
    q = h // 2
    return swap_z(down2[:h]), send_x(up2[h : h + q], 1), send_x(down2[h + q :], -1)


def with_core(pieces):
    return list(pieces) + [swap_core(piece) for piece in pieces]


def sum_cores(parts, kc):
    count = len(parts) // 2
    sent, got = list(parts[count:]), []
    for number in range(count):
        got.append(swap_core(sent[number]))
        if number + 1 < count:
            got[number], sent[number + 1] = after(got[number], sent[number + 1])
    steps = [mine + other for mine, other in zip(parts[:count], got)]
    pieces, sizes = [], [sum(entry[1] for entry in piece) for piece in shard_pieces(kc)]
    for step, numbers in zip(steps, ((7, 8, 9), (4, 5, 6), (0, 1, 2, 3))):
        base, cut = 0, []
        for number in numbers:
            cut.append(step[base : base + sizes[number]])
            base += sizes[number]
        pieces = cut + pieces
    return pieces


def third_back(z3, up3, down3):
    return swap_z(z3), send_x(up3, -1), send_x(down3, 1)


def second_back(z2, up2, down2, z3, up3, down3):
    h = z2.shape[0] // 2
    q = h // 2
    z2 = swap_z(z2)
    up2 = send_x(jnp.concatenate([up2[:h], up2[h : h + q] + up3, up2[h + q :]]), -1)
    down2 = send_x(jnp.concatenate([down2[:h] + z3, down2[h : h + q], down2[h + q :] + down3]), 1)
    return z2, up2, down2


def first_back(z1, up1, down1, z2, up2, down2):
    h = z2.shape[0] // 2
    z1 = swap_z(jnp.concatenate([z1[:h] + up2[h:] + down2[h:], z1[h:]]))
    up1 = send_x(up1 + jnp.concatenate([up2[:h], z2[:h]]), -1)
    down1 = send_x(jnp.concatenate([down1[:h], down1[h:] + down2[:h] + z2[h:]]), 1)
    return z1, up1, down1


def sum_rays(parts, far):
    first, near = parts[:NY], parts[NY] + far
    got = [col_shift(first[dy], 0, -dy) for dy in (1, 3, 2)]
    mine = first[0] + got[0] + got[1] + got[2]
    got = [col_shift(near[dy], 0, -dy) for dy in (1, 3, 2)]
    rest = near[0] + got[0] + got[1] + got[2]
    return mine[0] + col_shift(mine[1], 1, 0), rest


def spread_y(pair):
    return [pair] + [col_shift(pair, 0, dy) for dy in (1, 2, 3)]


def pad_row(row):
    return jnp.pad(row, (0, BS - row.shape[0]))[None]


def per_device(solution, residual, direction, gradient, blocks, block_rows, block_cols, counts):
    tile_blocks = blocks[0]
    width = direction.shape[1]
    kc = width
    sol, res, dirn, grad = solution.T, residual.T, direction.T, gradient.T
    row_index, col_index = lax.axis_index("row"), lax.axis_index("col")
    head = [
        counts[0, 0],
        row_index // 4,
        (row_index // 2) % 2,
        row_index % 2,
        col_index // 4,
        col_index % 4,
    ]
    head = jnp.stack(head + [jnp.int32(0)] * (HEAD - len(head))).astype(jnp.int32)
    lists = sorted_slots(block_rows[0], block_cols[0], head[0], head[1], head[2], head[3])
    meta = jnp.concatenate([head, lists])

    own = dirn
    first = first_step(own)
    first, meta = after(first, meta)
    own_other, z1_other = swap_core(own), swap_core(first[0])
    second = second_step(*first)
    ride, z1_other = after(res, z1_other)
    ride1, ride3 = col_shift(ride, 0, 1), col_shift(ride, 0, 3)
    second, ride1, ride3 = after(second, ride1, ride3)
    third = third_step(*second)
    others = [swap_core(piece) for piece in (*first[1:], *second)]
    ride, others = after(ride, others)
    ride2 = col_shift(ride, 0, 2)
    rides = jnp.stack([res, ride1, ride2, ride3])
    third, rides = after(third, rides)
    rides_z = col_shift(rides, 1, 0)
    others += [swap_core(piece) for piece in third]
    pieces = [own, *first, *second, *third, own_other, z1_other, *others]
    parts = forward(tile_blocks, meta, both_cores(kc), pieces, kc, (7, 14, 16))

    far = col_shift(parts[NY + 1], 1, 0)
    far, rides_z = after(far, rides_z)
    rides = [jnp.stack([rides[dy], rides_z[dy]]) for dy in range(NY)]
    image = jnp.concatenate(sum_rays(parts, far))
    norms = jnp.concatenate([jnp.sum(grad * grad, axis=1), jnp.sum(image * image, axis=1)])
    pair = jnp.stack([image, col_shift(image, 1, 0)])
    norms, pair = after(norms, pair)
    image_tile = spread_y(pair)
    norms = sum_over(norms[None], ("row", "col"))[0]
    gamma = norms[:width]
    alpha = (gamma / (norms[width:] + EPS))[:, None]
    back = backward(tile_blocks, meta, alpha, rides, image_tile, by_step(kc), kc, (4, 8, 12, 16))
    own_back, z1, up1, down1, z2, up2, down2, z3, up3, down3 = sum_cores(back, kc)
    third = third_back(z3, up3, down3)
    z2, third = after(z2, third)
    second = second_back(z2, up2, down2, *third)
    z1, up1, down1 = first_back(z1, up1, down1, *second)
    new_gradient = own_back + z1 + up1 + down1
    new_norms = jnp.sum(new_gradient * new_gradient, axis=1)
    new_norms = sum_over(pad_row(new_norms), ("row", "col"))[0, :width]
    beta = (new_norms / gamma)[:, None]
    return (sol + alpha * dirn).T, (res - alpha * image).T, (new_gradient + beta * dirn).T


def solution(mesh):
    placed = (
        P(("col", "row"), None),
        P(("row", "col"), None),
        P(("col", "row"), None),
        P(("col", "row"), None),
        P("row", "col", None, None),
        P("row", "col"),
        P("row", "col"),
        P("row", "col"),
    )
    return jax.shard_map(
        per_device,
        mesh=mesh,
        in_specs=placed,
        out_specs=(P(("col", "row"), None), P(("row", "col"), None), P(("col", "row"), None)),
        check_vma=False,
    )
```

```python
import functools

import jax
import jax.numpy as jnp
from jax import lax
from jax.experimental import pallas as pl
from jax.experimental.pallas import tpu as pltpu
from jax.sharding import PartitionSpec as P

EPS = 1e-06
BS = 128
GROUP = 16
HEAD = 8
NEAR = ((0, 0), (0, 1), (3, 0), (1, 0), (2, 0), (3, 1), (1, 1))
SEQUENCE = tuple((dx, dz, dc) for dc in (0, 1) for dx, dz in NEAR) + ((2, 1, 0), (2, 1, 1))
YROWS = 40
BUFFERS = 6
VMEM_BYTES = 32 * 1024 * 1024

NX, NZ, NCORE = 4, 2, 2
NZH, NY = 2, 4


def row_of(x, z, c):
    return (x % NX) * 4 + (z % NZ) * 2 + c % NCORE


def col_of(z, y):
    return (z % NZH) * 4 + y % NY


def row_shift(value, dx, dz, dc):
    pairs = [
        (row_of(x + dx, z + dz, c + dc), row_of(x, z, c))
        for x in range(NX)
        for z in range(NZ)
        for c in range(NCORE)
    ]
    return lax.ppermute(value, "row", pairs)


def col_shift(value, dz, dy):
    pairs = [(col_of(z + dz, y + dy), col_of(z, y)) for z in range(NZH) for y in range(NY)]
    return lax.ppermute(value, "col", pairs)


def sum_over(row, axes):
    count = lax.axis_size(axes)
    sent = jnp.broadcast_to(row[None], (count, 1, row.shape[1]))
    return jnp.sum(lax.all_to_all(sent, axes, 0, 0, tiled=True), axis=0)


def split(value):
    high = value.astype(jnp.bfloat16)
    low = (value - high.astype(jnp.float32)).astype(jnp.bfloat16)
    return high, low


def doubled(value):
    high, low = split(value)
    return jnp.concatenate(
        [jnp.concatenate([high, high], axis=1), jnp.concatenate([low, low], axis=1)], axis=0
    )


def fetch(blocks, held, sems, meta_ref, group):
    buffer = group % BUFFERS
    for inner in range(GROUP):
        slot = meta_ref[HEAD + group * GROUP + inner]
        pltpu.make_async_copy(blocks.at[slot], held.at[buffer, inner], sems.at[buffer]).start()


def run_groups(blocks, held, sems, meta_ref, start, stop, total, work):
    def one(group, _):
        buffer = group % BUFFERS
        pltpu.make_async_copy(blocks.at[pl.ds(0, GROUP)], held.at[buffer], sems.at[buffer]).wait()
        work(group, buffer)

        @pl.when(group + BUFFERS < total)
        def _():
            fetch(blocks, held, sems, meta_ref, group + BUFFERS)

        return 0

    lax.fori_loop(start, stop, one, 0)


def fetch_first(blocks, held, sems, meta_ref, total):
    def one(group, _):
        fetch(blocks, held, sems, meta_ref, group)
        return 0

    lax.fori_loop(0, jnp.minimum(total, BUFFERS), one, 0)


def ends_of(meta_ref, slots, position):
    return meta_ref[HEAD + 3 * (slots + GROUP) + position]


def owner_of(meta_ref, place):
    dx, dz, dc = place
    x, z, c = meta_ref[1], meta_ref[2], meta_ref[3]
    return ((x + dx) % NX) * 4 + ((z + dz) % NZ) * 2 + (c + dc) % NCORE


def forward_kernel(kc, slots, stages, places, meta_ref, blocks_ref, *refs):
    pieces = refs[: len(places)]
    outs = refs[len(places) : len(places) + NY + NZH]
    acc, panel, held, sems, block_sems = refs[len(places) + NY + NZH :]
    last = ends_of(meta_ref, slots, len(SEQUENCE) - 1)
    total = (last + GROUP - 1) // GROUP

    copies = []
    for number, (dc, entries) in enumerate(places):
        for source, size, (dx, dz), start in entries:
            position = SEQUENCE.index((dx, dz, dc))
            copy = pltpu.make_async_copy(
                pieces[number].at[pl.ds(source, size)],
                panel.at[position, pl.ds(start, size), :],
                sems.at[len(copies)],
            )
            copies.append((position, copy))
    for _, copy in copies:
        copy.start()
    fetch_first(blocks_ref, held, block_sems, meta_ref, total)
    acc[...] = jnp.zeros_like(acc)

    def work(group, buffer):
        for inner in range(GROUP):
            slot = group * GROUP + inner
            place = meta_ref[HEAD + 2 * (slots + GROUP) + slot]
            offset = pl.multiple_of((place % 32) * BS, BS)
            left = doubled(panel[place // 32, :, pl.ds(offset, BS)])
            high, low = split(held[buffer, inner])
            right = jnp.concatenate([high, low], axis=1)
            both = lax.dot_general(
                right, left, (((1,), (1,)), ((), ())), preferred_element_type=jnp.float32
            )
            live = jnp.where(slot < last, 1.0, 0.0)
            acc[meta_ref[HEAD + slots + GROUP + slot]] += both * live

    done, waited = 0, 0
    for stage in stages:
        for position, copy in copies:
            if waited <= position < stage:
                copy.wait()
        waited = stage
        stop = total if stage == stages[-1] else ends_of(meta_ref, slots, stage - 1) // GROUP
        run_groups(blocks_ref, held, block_sems, meta_ref, done, stop, total, work)
        done = stop

    zh, y = meta_ref[4], meta_ref[5]
    per = acc.shape[0] // (NZH * NY)
    for dy in range(NY):
        for dz in range(NZH):
            piece = ((zh + dz) % NZH) * 4 + (y + dy) % NY
            for t in range(per):
                both = acc[piece * per + t].T
                both = both[:kc] + both[kc:]
                outs[dy][dz, :, t * BS : (t + 1) * BS] = both[:YROWS]
                outs[NY + dz][dy, :, t * BS : (t + 1) * BS] = both[YROWS:]


def backward_kernel(kc, slots, stages, layout, meta_ref, blocks_ref, alpha_ref, *refs):
    res = refs[:NY]
    img = refs[NY : 2 * NY]
    outs = refs[2 * NY : 2 * NY + len(layout)]
    source, acc, held, sems, block_sems = refs[2 * NY + len(layout) :]
    last = ends_of(meta_ref, slots, len(SEQUENCE) - 1)
    total = (last + GROUP - 1) // GROUP
    fetch_first(blocks_ref, held, block_sems, meta_ref, total)

    zh, y = meta_ref[4], meta_ref[5]
    per = source.shape[0] // (NZH * NY)
    alpha = alpha_ref[...]
    for dy in range(NY):
        for dz in range(NZH):
            piece = ((zh + dz) % NZH) * 4 + (y + dy) % NY
            for t in range(per):
                span = slice(t * BS, (t + 1) * BS)
                value = res[dy][dz, :, span] - alpha * img[dy][dz, :, span]
                source[piece * per + t] = doubled(value)

    def clear(i, _):
        acc[i] = jnp.zeros(acc.shape[1:], jnp.float32)
        return 0

    lax.fori_loop(0, acc.shape[0], clear, 0)

    def work(group, buffer):
        for inner in range(GROUP):
            slot = group * GROUP + inner
            left = source[meta_ref[HEAD + slots + GROUP + slot]]
            high, low = split(held[buffer, inner])
            right = jnp.concatenate([high, low], axis=0)
            both = lax.dot_general(
                left, right, (((1,), (0,)), ((), ())), preferred_element_type=jnp.float32
            )
            live = jnp.where(slot < last, 1.0, 0.0)
            place = meta_ref[HEAD + 2 * (slots + GROUP) + slot]
            offset = pl.multiple_of((place % 32) * BS, BS)
            acc[place // 32, :, pl.ds(offset, BS)] += (both[:kc] + both[kc:]) * live

    copies = []
    for number, (dc, entries) in enumerate(layout):
        for target, size, (dx, dz), start in entries:
            position = SEQUENCE.index((dx, dz, dc))
            copy = pltpu.make_async_copy(
                acc.at[position, pl.ds(start, size), :],
                outs[number].at[pl.ds(target, size)],
                sems.at[len(copies)],
            )
            copies.append((position, copy))
    done, sent = 0, 0
    for stage in stages:
        stop = (ends_of(meta_ref, slots, stage - 1) + GROUP - 1) // GROUP
        run_groups(blocks_ref, held, block_sems, meta_ref, done, stop, total, work)
        done = stop
        for position, copy in copies:
            if sent <= position < stage:
                copy.start()
        sent = stage
    for _, copy in copies:
        copy.wait()


def cost(kc, slots, shards):
    return pl.CostEstimate(
        flops=6 * slots * BS * BS * kc,
        bytes_accessed=4 * (slots * BS * BS + 2 * shards * kc * 4096),
        transcendentals=0,
    )


def forward(blocks, meta, places, pieces, kc, stages):
    slots = blocks.shape[0]
    smem, vmem = pl.BlockSpec(memory_space=pltpu.SMEM), pl.BlockSpec(memory_space=pltpu.VMEM)
    any_spec = pl.BlockSpec(memory_space=pl.ANY)
    out_shape = [jax.ShapeDtypeStruct((NZH, YROWS, 6 * BS), jnp.float32)] * NY
    out_shape += [jax.ShapeDtypeStruct((NY, kc - YROWS, 6 * BS), jnp.float32)] * NZH
    return pl.pallas_call(
        functools.partial(forward_kernel, kc, slots, stages, places),
        in_specs=[smem] + [any_spec] * (1 + len(pieces)),
        out_specs=[vmem] * len(out_shape),
        scratch_shapes=[
            pltpu.VMEM((48, BS, 2 * kc), jnp.float32),
            pltpu.VMEM((16, kc, 4096), jnp.float32),
            pltpu.VMEM((BUFFERS, GROUP, BS, BS), jnp.float32),
            pltpu.SemaphoreType.DMA((sum(len(entries) for _, entries in places),)),
            pltpu.SemaphoreType.DMA((BUFFERS,)),
        ],
        out_shape=out_shape,
        compiler_params=pltpu.CompilerParams(vmem_limit_bytes=VMEM_BYTES),
        cost_estimate=cost(kc, slots, len(SEQUENCE)),
    )(meta, blocks, *pieces)


def backward(blocks, meta, alpha, res, img, layout, kc, stages):
    slots = blocks.shape[0]
    smem, vmem = pl.BlockSpec(memory_space=pltpu.SMEM), pl.BlockSpec(memory_space=pltpu.VMEM)
    any_spec = pl.BlockSpec(memory_space=pl.ANY)
    shapes = [(sum(entry[1] for entry in entries), 4096) for _, entries in layout]
    return pl.pallas_call(
        functools.partial(backward_kernel, kc, slots, stages, layout),
        in_specs=[smem] + [any_spec] + [vmem] * (1 + 2 * NY),
        out_specs=[any_spec] * len(layout),
        scratch_shapes=[
            pltpu.VMEM((48, 2 * kc, 2 * BS), jnp.bfloat16),
            pltpu.VMEM((16, kc, 4096), jnp.float32),
            pltpu.VMEM((BUFFERS, GROUP, BS, BS), jnp.float32),
            pltpu.SemaphoreType.DMA((sum(len(entries) for _, entries in layout),)),
            pltpu.SemaphoreType.DMA((BUFFERS,)),
        ],
        out_shape=[jax.ShapeDtypeStruct(shape, jnp.float32) for shape in shapes],
        compiler_params=pltpu.CompilerParams(vmem_limit_bytes=VMEM_BYTES),
        cost_estimate=cost(kc, slots, len(SEQUENCE)),
    )(meta, blocks, alpha, *res, *img)


def sorted_slots(rows, cols, count, x, z, c):
    slots = rows.shape[0]
    number = jnp.arange(slots, dtype=jnp.int32)
    owner = cols // 32
    code = ((owner // 4 - x) % NX) * 4 + ((owner // 2 - z) % NZ) * 2 + (owner - c) % NCORE
    codes = jnp.array([dx * 4 + dz * 2 + dc for dx, dz, dc in SEQUENCE], jnp.int32)
    steps = jnp.arange(len(SEQUENCE), dtype=jnp.int32)
    position = jnp.sum(jnp.where(code[:, None] == codes, steps, 0), axis=1)
    live = number < count
    key = jnp.where(live, position, len(SEQUENCE)) * slots + number
    rank = jnp.sum((key[None] < key[:, None]).astype(jnp.int32), axis=1)
    where = rank[None] == number[:, None]
    place = position * 32 + cols % 32
    lists = [jnp.sum(jnp.where(where, value[None], 0), axis=1) for value in (number, rows, place)]
    ends = jnp.sum((live[None] & (position[None] <= steps[:, None])).astype(jnp.int32), axis=1)
    pad = jnp.zeros((GROUP,), jnp.int32)
    return jnp.concatenate([part for value in lists for part in (value, pad)] + [ends])


def after(*values):
    return lax.optimization_barrier(values)


def swap_core(value):
    return row_shift(value, 0, 0, 1)


def swap_z(value):
    return row_shift(value, 0, 1, 0)


def send_x(value, step):
    return row_shift(value, -step, 0, 0)


def third_rows(kc):
    return 3 * kc // 8


def shard_pieces(kc):
    h, t = kc // 2, third_rows(kc)
    return (
        ((0, kc, (0, 0), 0),),
        ((0, kc, (0, 1), 0),),
        ((0, kc, (3, 0), 0),),
        ((0, kc, (1, 0), 0),),
        ((0, h, (3, 1), h), (h, h, (1, 1), h)),
        ((0, h, (2, 0), 0), (h, h, (3, 1), 0)),
        ((0, h, (2, 0), h), (h, h, (1, 1), 0)),
        ((0, kc - 2 * t, (2, 1), 2 * t),),
        ((0, t, (2, 1), 0),),
        ((0, t, (2, 1), t),),
    )


def both_cores(kc):
    return tuple((dc, entries) for dc in range(NCORE) for entries in shard_pieces(kc))


def by_step(kc):
    pieces = shard_pieces(kc)
    layout = []
    for dc in range(NCORE):
        for step in (pieces[7:], pieces[4:7], pieces[:4]):
            entries, base = [], 0
            for piece in step:
                entries += [(base + first, size, owner, start) for first, size, owner, start in piece]
                base += sum(entry[1] for entry in piece)
            layout.append((dc, tuple(entries)))
    return tuple(layout)


def first_step(own):
    return swap_z(own), send_x(own, 1), send_x(own, -1)


def second_step(z1, up1, down1):
    h = z1.shape[0] // 2
    z2 = swap_z(jnp.concatenate([up1[h:], down1[h:]]))
    up2 = send_x(jnp.concatenate([up1[:h], z1[:h]]), 1)
    down2 = send_x(jnp.concatenate([down1[h:], z1[:h]]), -1)
    return z2, up2, down2


def third_step(z2, up2, down2):
    h, t = z2.shape[0] // 2, third_rows(z2.shape[0])
    down3 = jnp.concatenate([down2[h + t :], z2[h : 2 * t]])
    return swap_z(down2[2 * t - h : h]), send_x(up2[h : h + t], 1), send_x(down3, -1)


def with_core(pieces):
    return list(pieces) + [swap_core(piece) for piece in pieces]


def sum_cores(parts, kc):
    count = len(parts) // 2
    sent, got = list(parts[count:]), []
    for number in range(count):
        got.append(swap_core(sent[number]))
        if number + 1 < count:
            got[number], sent[number + 1] = after(got[number], sent[number + 1])
    steps = [mine + other for mine, other in zip(parts[:count], got)]
    pieces, sizes = [], [sum(entry[1] for entry in piece) for piece in shard_pieces(kc)]
    for step, numbers in zip(steps, ((7, 8, 9), (4, 5, 6), (0, 1, 2, 3))):
        base, cut = 0, []
        for number in numbers:
            cut.append(step[base : base + sizes[number]])
            base += sizes[number]
        pieces = cut + pieces
    return pieces


def third_back(z3, up3, down3):
    return swap_z(z3), send_x(up3, -1), send_x(down3, 1)


def second_back(z2, up2, down2, z3, up3, down3):
    h, t = z2.shape[0] // 2, third_rows(z2.shape[0])
    z2 = jnp.concatenate([z2[:h], z2[h : 2 * t] + down3[h - t :], z2[2 * t :]])
    up2 = jnp.concatenate([up2[:h], up2[h : h + t] + up3, up2[h + t :]])
    down2 = jnp.concatenate(
        [
            down2[: 2 * t - h],
            down2[2 * t - h : h] + z3,
            down2[h : h + t],
            down2[h + t :] + down3[: h - t],
        ]
    )
    return swap_z(z2), send_x(up2, -1), send_x(down2, 1)


def first_back(z1, up1, down1, z2, up2, down2):
    h = z2.shape[0] // 2
    z1 = swap_z(jnp.concatenate([z1[:h] + up2[h:] + down2[h:], z1[h:]]))
    up1 = send_x(up1 + jnp.concatenate([up2[:h], z2[:h]]), -1)
    down1 = send_x(jnp.concatenate([down1[:h], down1[h:] + down2[:h] + z2[h:]]), 1)
    return z1, up1, down1


def sum_rays(parts, far):
    first, near = parts[:NY], parts[NY] + far
    got = [col_shift(first[dy], 0, -dy) for dy in (1, 3, 2)]
    mine = first[0] + got[0] + got[1] + got[2]
    got = [col_shift(near[dy], 0, -dy) for dy in (1, 3, 2)]
    rest = near[0] + got[0] + got[1] + got[2]
    return mine[0] + col_shift(mine[1], 1, 0), rest


def spread_y(pair):
    return [pair] + [col_shift(pair, 0, dy) for dy in (1, 2, 3)]


def pad_row(row):
    return jnp.pad(row, (0, BS - row.shape[0]))[None]


def per_device(solution, residual, direction, gradient, blocks, block_rows, block_cols, counts):
    tile_blocks = blocks[0]
    width = direction.shape[1]
    kc = width
    sol, res, dirn, grad = solution.T, residual.T, direction.T, gradient.T
    row_index, col_index = lax.axis_index("row"), lax.axis_index("col")
    head = [
        counts[0, 0],
        row_index // 4,
        (row_index // 2) % 2,
        row_index % 2,
        col_index // 4,
        col_index % 4,
    ]
    head = jnp.stack(head + [jnp.int32(0)] * (HEAD - len(head))).astype(jnp.int32)
    lists = sorted_slots(block_rows[0], block_cols[0], head[0], head[1], head[2], head[3])
    meta = jnp.concatenate([head, lists])

    own = dirn
    first = first_step(own)
    own_other = swap_core(own)
    ride, own_other = after(res, own_other)
    ride1, ride3 = col_shift(ride, 0, 1), col_shift(ride, 0, 3)
    first, meta, ride1, ride3 = after(first, meta, ride1, ride3)
    z1_other = swap_core(first[0])
    second = second_step(*first)
    ride, z1_other = after(ride, z1_other)
    ride2 = col_shift(ride, 0, 2)
    second, ride2 = after(second, ride2)
    third = third_step(*second)
    others = [swap_core(piece) for piece in (*first[1:], *second)]
    rides = jnp.stack([res, ride1, ride2, ride3])
    rides, third_x = after(rides, third[1:])
    third = (third[0], *third_x)
    rides_z = col_shift(rides, 1, 0)
    others += [swap_core(piece) for piece in third]
    pieces = [own, *first, *second, *third, own_other, z1_other, *others]
    parts = forward(tile_blocks, meta, both_cores(kc), pieces, kc, (7, 14, 16))

    far = col_shift(parts[NY + 1], 1, 0)
    far, rides_z = after(far, rides_z)
    rides = [jnp.stack([rides[dy], rides_z[dy]]) for dy in range(NY)]
    image = jnp.concatenate(sum_rays(parts, far))
    norms = jnp.concatenate([jnp.sum(grad * grad, axis=1), jnp.sum(image * image, axis=1)])
    pair = jnp.stack([image, col_shift(image, 1, 0)])
    norms, pair = after(norms, pair)
    image_tile = spread_y(pair)
    norms = sum_over(norms[None], ("row", "col"))[0]
    gamma = norms[:width]
    alpha = (gamma / (norms[width:] + EPS))[:, None]
    back = backward(tile_blocks, meta, alpha, rides, image_tile, by_step(kc), kc, (4, 8, 12, 16))
    own_back, z1, up1, down1, z2, up2, down2, z3, up3, down3 = sum_cores(back, kc)
    third = third_back(z3, up3, down3)
    z2, third = after(z2, third)
    second = second_back(z2, up2, down2, *third)
    z1, up1, down1 = first_back(z1, up1, down1, *second)
    new_gradient = own_back + z1 + up1 + down1
    new_norms = jnp.sum(new_gradient * new_gradient, axis=1)
    new_norms = sum_over(pad_row(new_norms), ("row", "col"))[0, :width]
    beta = (new_norms / gamma)[:, None]
    return (sol + alpha * dirn).T, (res - alpha * image).T, (new_gradient + beta * dirn).T


def solution(mesh):
    placed = (
        P(("col", "row"), None),
        P(("row", "col"), None),
        P(("col", "row"), None),
        P(("col", "row"), None),
        P("row", "col", None, None),
        P("row", "col"),
        P("row", "col"),
        P("row", "col"),
    )
    return jax.shard_map(
        per_device,
        mesh=mesh,
        in_specs=placed,
        out_specs=(P(("col", "row"), None), P(("row", "col"), None), P(("col", "row"), None)),
        check_vma=False,
    )
```

```python
import functools

import jax
import jax.numpy as jnp
from jax import lax
from jax.experimental import pallas as pl
from jax.experimental.pallas import tpu as pltpu
from jax.sharding import PartitionSpec as P

EPS = 1e-06
BS = 128
GROUP = 16
HEAD = 8
NEAR = ((0, 0), (0, 1), (3, 0), (1, 0), (2, 0), (3, 1), (1, 1))
SEQUENCE = tuple((dx, dz, dc) for dc in (0, 1) for dx, dz in NEAR) + ((2, 1, 0), (2, 1, 1))
YROWS = 40
BUFFERS = 6
VMEM_BYTES = 32 * 1024 * 1024

NX, NZ, NCORE = 4, 2, 2
NZH, NY = 2, 4


def row_of(x, z, c):
    return (x % NX) * 4 + (z % NZ) * 2 + c % NCORE


def col_of(z, y):
    return (z % NZH) * 4 + y % NY


def row_shift(value, dx, dz, dc):
    pairs = [
        (row_of(x + dx, z + dz, c + dc), row_of(x, z, c))
        for x in range(NX)
        for z in range(NZ)
        for c in range(NCORE)
    ]
    return lax.ppermute(value, "row", pairs)


def col_shift(value, dz, dy):
    pairs = [(col_of(z + dz, y + dy), col_of(z, y)) for z in range(NZH) for y in range(NY)]
    return lax.ppermute(value, "col", pairs)


def sum_over(row, axes):
    count = lax.axis_size(axes)
    sent = jnp.broadcast_to(row[None], (count, 1, row.shape[1]))
    return jnp.sum(lax.all_to_all(sent, axes, 0, 0, tiled=True), axis=0)


def split(value):
    high = value.astype(jnp.bfloat16)
    low = (value - high.astype(jnp.float32)).astype(jnp.bfloat16)
    return high, low


def doubled(value):
    high, low = split(value)
    return jnp.concatenate(
        [jnp.concatenate([high, high], axis=1), jnp.concatenate([low, low], axis=1)], axis=0
    )


def fetch(blocks, held, sems, meta_ref, group):
    buffer = group % BUFFERS
    for inner in range(GROUP):
        slot = meta_ref[HEAD + group * GROUP + inner]
        pltpu.make_async_copy(blocks.at[slot], held.at[buffer, inner], sems.at[buffer]).start()


def run_groups(blocks, held, sems, meta_ref, start, stop, total, work):
    def one(group, _):
        buffer = group % BUFFERS
        pltpu.make_async_copy(blocks.at[pl.ds(0, GROUP)], held.at[buffer], sems.at[buffer]).wait()
        work(group, buffer)

        @pl.when(group + BUFFERS < total)
        def _():
            fetch(blocks, held, sems, meta_ref, group + BUFFERS)

        return 0

    lax.fori_loop(start, stop, one, 0)


def fetch_first(blocks, held, sems, meta_ref, total):
    def one(group, _):
        fetch(blocks, held, sems, meta_ref, group)
        return 0

    lax.fori_loop(0, jnp.minimum(total, BUFFERS), one, 0)


def ends_of(meta_ref, slots, position):
    return meta_ref[HEAD + 3 * (slots + GROUP) + position]


def owner_of(meta_ref, place):
    dx, dz, dc = place
    x, z, c = meta_ref[1], meta_ref[2], meta_ref[3]
    return ((x + dx) % NX) * 4 + ((z + dz) % NZ) * 2 + (c + dc) % NCORE


def turn_kernel(blocks_ref, out_ref, taken, turned, in_sems, out_sems):
    depth = taken.shape[0]
    total = blocks_ref.shape[0] // GROUP

    def take(chunk):
        span = pl.ds(chunk * GROUP, GROUP)
        buffer = chunk % depth
        return pltpu.make_async_copy(blocks_ref.at[span], taken.at[buffer], in_sems.at[buffer])

    def give(chunk):
        span = pl.ds(chunk * GROUP, GROUP)
        buffer = chunk % depth
        return pltpu.make_async_copy(turned.at[buffer], out_ref.at[span], out_sems.at[buffer])

    for chunk in range(depth):
        take(chunk).start()

    def work(chunk, _):
        buffer = chunk % depth
        take(chunk).wait()

        @pl.when(chunk >= depth)
        def _():
            give(chunk - depth).wait()

        for inner in range(GROUP):
            high, low = split(taken[buffer, inner].T)
            turned[buffer, inner, :BS] = high
            turned[buffer, inner, BS:] = low
        give(chunk).start()

        @pl.when(chunk + depth < total)
        def _():
            take(chunk + depth).start()

        return 0

    lax.fori_loop(0, total, work, 0)
    for chunk in range(total - depth, total):
        give(chunk).wait()


def turn_blocks(blocks):
    depth = 4
    shape = (blocks.shape[0], 2 * BS, BS)
    return pl.pallas_call(
        turn_kernel,
        in_specs=[pl.BlockSpec(memory_space=pltpu.HBM)],
        out_specs=pl.BlockSpec(memory_space=pltpu.HBM),
        scratch_shapes=[
            pltpu.VMEM((depth, GROUP, BS, BS), jnp.float32),
            pltpu.VMEM((depth, GROUP, 2 * BS, BS), jnp.bfloat16),
            pltpu.SemaphoreType.DMA((depth,)),
            pltpu.SemaphoreType.DMA((depth,)),
        ],
        out_shape=jax.ShapeDtypeStruct(shape, jnp.bfloat16),
        compiler_params=pltpu.CompilerParams(vmem_limit_bytes=16 * 1024 * 1024),
        cost_estimate=pl.CostEstimate(
            flops=0, bytes_accessed=8 * blocks.size, transcendentals=0
        ),
    )(blocks)


def forward_kernel(kc, slots, stages, places, meta_ref, blocks_ref, *refs):
    pieces = refs[: len(places)]
    outs = refs[len(places) : len(places) + NY + NZH]
    acc, panel, held, sems, block_sems = refs[len(places) + NY + NZH :]
    last = ends_of(meta_ref, slots, len(SEQUENCE) - 1)
    total = (last + GROUP - 1) // GROUP

    copies = []
    for number, (dc, entries) in enumerate(places):
        for source, size, (dx, dz), start in entries:
            position = SEQUENCE.index((dx, dz, dc))
            copy = pltpu.make_async_copy(
                pieces[number].at[pl.ds(source, size)],
                panel.at[position, pl.ds(start, size), :],
                sems.at[len(copies)],
            )
            copies.append((position, copy))
    for _, copy in copies:
        copy.start()
    fetch_first(blocks_ref, held, block_sems, meta_ref, total)
    acc[...] = jnp.zeros_like(acc)

    def work(group, buffer):
        for inner in range(GROUP):
            slot = group * GROUP + inner
            place = meta_ref[HEAD + 2 * (slots + GROUP) + slot]
            offset = pl.multiple_of((place % 32) * BS, BS)
            both = jnp.dot(
                doubled(panel[place // 32, :, pl.ds(offset, BS)]),
                held[buffer, inner],
                preferred_element_type=jnp.float32,
            )
            live = jnp.where(slot < last, 1.0, 0.0)
            acc[meta_ref[HEAD + slots + GROUP + slot]] += (both[:kc] + both[kc:]) * live

    done, waited = 0, 0
    for stage in stages:
        for position, copy in copies:
            if waited <= position < stage:
                copy.wait()
        waited = stage
        stop = total if stage == stages[-1] else ends_of(meta_ref, slots, stage - 1) // GROUP
        run_groups(blocks_ref, held, block_sems, meta_ref, done, stop, total, work)
        done = stop

    zh, y = meta_ref[4], meta_ref[5]
    per = acc.shape[0] // (NZH * NY)
    for dy in range(NY):
        for dz in range(NZH):
            piece = ((zh + dz) % NZH) * 4 + (y + dy) % NY
            for t in range(per):
                both = acc[piece * per + t]
                outs[dy][dz, :, t * BS : (t + 1) * BS] = both[:YROWS]
                outs[NY + dz][dy, :, t * BS : (t + 1) * BS] = both[YROWS:]


def backward_kernel(kc, slots, stages, layout, meta_ref, blocks_ref, alpha_ref, *refs):
    res = refs[:NY]
    img = refs[NY : 2 * NY]
    outs = refs[2 * NY : 2 * NY + len(layout)]
    source, acc, held, sems, block_sems = refs[2 * NY + len(layout) :]
    last = ends_of(meta_ref, slots, len(SEQUENCE) - 1)
    total = (last + GROUP - 1) // GROUP
    fetch_first(blocks_ref, held, block_sems, meta_ref, total)

    zh, y = meta_ref[4], meta_ref[5]
    per = source.shape[0] // (NZH * NY)
    alpha = alpha_ref[...]
    for dy in range(NY):
        for dz in range(NZH):
            piece = ((zh + dz) % NZH) * 4 + (y + dy) % NY
            for t in range(per):
                span = slice(t * BS, (t + 1) * BS)
                value = res[dy][dz, :, span] - alpha * img[dy][dz, :, span]
                source[piece * per + t] = doubled(value)

    def clear(i, _):
        acc[i] = jnp.zeros(acc.shape[1:], jnp.float32)
        return 0

    lax.fori_loop(0, acc.shape[0], clear, 0)

    def work(group, buffer):
        for inner in range(GROUP):
            slot = group * GROUP + inner
            left = source[meta_ref[HEAD + slots + GROUP + slot]]
            high, low = split(held[buffer, inner])
            right = jnp.concatenate([high, low], axis=0)
            both = lax.dot_general(
                left, right, (((1,), (0,)), ((), ())), preferred_element_type=jnp.float32
            )
            live = jnp.where(slot < last, 1.0, 0.0)
            place = meta_ref[HEAD + 2 * (slots + GROUP) + slot]
            offset = pl.multiple_of((place % 32) * BS, BS)
            acc[place // 32, :, pl.ds(offset, BS)] += (both[:kc] + both[kc:]) * live

    copies = []
    for number, (dc, entries) in enumerate(layout):
        for target, size, (dx, dz), start in entries:
            position = SEQUENCE.index((dx, dz, dc))
            copy = pltpu.make_async_copy(
                acc.at[position, pl.ds(start, size), :],
                outs[number].at[pl.ds(target, size)],
                sems.at[len(copies)],
            )
            copies.append((position, copy))
    done, sent = 0, 0
    for stage in stages:
        stop = (ends_of(meta_ref, slots, stage - 1) + GROUP - 1) // GROUP
        run_groups(blocks_ref, held, block_sems, meta_ref, done, stop, total, work)
        done = stop
        for position, copy in copies:
            if sent <= position < stage:
                copy.start()
        sent = stage
    for _, copy in copies:
        copy.wait()


def cost(kc, slots, shards):
    return pl.CostEstimate(
        flops=6 * slots * BS * BS * kc,
        bytes_accessed=4 * (slots * BS * BS + 2 * shards * kc * 4096),
        transcendentals=0,
    )


def forward(blocks, meta, places, pieces, kc, stages):
    slots = blocks.shape[0]
    smem, vmem = pl.BlockSpec(memory_space=pltpu.SMEM), pl.BlockSpec(memory_space=pltpu.VMEM)
    any_spec = pl.BlockSpec(memory_space=pl.ANY)
    out_shape = [jax.ShapeDtypeStruct((NZH, YROWS, 6 * BS), jnp.float32)] * NY
    out_shape += [jax.ShapeDtypeStruct((NY, kc - YROWS, 6 * BS), jnp.float32)] * NZH
    return pl.pallas_call(
        functools.partial(forward_kernel, kc, slots, stages, places),
        in_specs=[smem, pl.BlockSpec(memory_space=pltpu.HBM)] + [any_spec] * len(pieces),
        out_specs=[vmem] * len(out_shape),
        scratch_shapes=[
            pltpu.VMEM((48, kc, BS), jnp.float32),
            pltpu.VMEM((16, kc, 4096), jnp.float32),
            pltpu.VMEM((BUFFERS, GROUP, 2 * BS, BS), jnp.bfloat16),
            pltpu.SemaphoreType.DMA((sum(len(entries) for _, entries in places),)),
            pltpu.SemaphoreType.DMA((BUFFERS,)),
        ],
        out_shape=out_shape,
        compiler_params=pltpu.CompilerParams(vmem_limit_bytes=VMEM_BYTES),
        cost_estimate=cost(kc, slots, len(SEQUENCE)),
    )(meta, blocks, *pieces)


def backward(blocks, meta, alpha, res, img, layout, kc, stages):
    slots = blocks.shape[0]
    smem, vmem = pl.BlockSpec(memory_space=pltpu.SMEM), pl.BlockSpec(memory_space=pltpu.VMEM)
    any_spec = pl.BlockSpec(memory_space=pl.ANY)
    shapes = [(sum(entry[1] for entry in entries), 4096) for _, entries in layout]
    return pl.pallas_call(
        functools.partial(backward_kernel, kc, slots, stages, layout),
        in_specs=[smem] + [any_spec] + [vmem] * (1 + 2 * NY),
        out_specs=[any_spec] * len(layout),
        scratch_shapes=[
            pltpu.VMEM((48, 2 * kc, 2 * BS), jnp.bfloat16),
            pltpu.VMEM((16, kc, 4096), jnp.float32),
            pltpu.VMEM((BUFFERS, GROUP, BS, BS), jnp.float32),
            pltpu.SemaphoreType.DMA((sum(len(entries) for _, entries in layout),)),
            pltpu.SemaphoreType.DMA((BUFFERS,)),
        ],
        out_shape=[jax.ShapeDtypeStruct(shape, jnp.float32) for shape in shapes],
        compiler_params=pltpu.CompilerParams(vmem_limit_bytes=VMEM_BYTES),
        cost_estimate=cost(kc, slots, len(SEQUENCE)),
    )(meta, blocks, alpha, *res, *img)


def sorted_slots(rows, cols, count, x, z, c):
    slots = rows.shape[0]
    number = jnp.arange(slots, dtype=jnp.int32)
    owner = cols // 32
    code = ((owner // 4 - x) % NX) * 4 + ((owner // 2 - z) % NZ) * 2 + (owner - c) % NCORE
    codes = jnp.array([dx * 4 + dz * 2 + dc for dx, dz, dc in SEQUENCE], jnp.int32)
    steps = jnp.arange(len(SEQUENCE), dtype=jnp.int32)
    position = jnp.sum(jnp.where(code[:, None] == codes, steps, 0), axis=1)
    live = number < count
    key = jnp.where(live, position, len(SEQUENCE)) * slots + number
    rank = jnp.sum((key[None] < key[:, None]).astype(jnp.int32), axis=1)
    where = rank[None] == number[:, None]
    place = position * 32 + cols % 32
    lists = [jnp.sum(jnp.where(where, value[None], 0), axis=1) for value in (number, rows, place)]
    ends = jnp.sum((live[None] & (position[None] <= steps[:, None])).astype(jnp.int32), axis=1)
    pad = jnp.zeros((GROUP,), jnp.int32)
    return jnp.concatenate([part for value in lists for part in (value, pad)] + [ends])


def after(*values):
    return lax.optimization_barrier(values)


def swap_core(value):
    return row_shift(value, 0, 0, 1)


def swap_z(value):
    return row_shift(value, 0, 1, 0)


def send_x(value, step):
    return row_shift(value, -step, 0, 0)


def third_rows(kc):
    return 3 * kc // 8


def shard_pieces(kc):
    h, t = kc // 2, third_rows(kc)
    return (
        ((0, kc, (0, 0), 0),),
        ((0, kc, (0, 1), 0),),
        ((0, kc, (3, 0), 0),),
        ((0, kc, (1, 0), 0),),
        ((0, h, (3, 1), h), (h, h, (1, 1), h)),
        ((0, h, (2, 0), 0), (h, h, (3, 1), 0)),
        ((0, h, (2, 0), h), (h, h, (1, 1), 0)),
        ((0, kc - 2 * t, (2, 1), 2 * t),),
        ((0, t, (2, 1), 0),),
        ((0, t, (2, 1), t),),
    )


def both_cores(kc):
    return tuple((dc, entries) for dc in range(NCORE) for entries in shard_pieces(kc))


def by_step(kc):
    pieces = shard_pieces(kc)
    layout = []
    for dc in range(NCORE):
        for step in (pieces[7:], pieces[4:7], pieces[:4]):
            entries, base = [], 0
            for piece in step:
                entries += [(base + first, size, owner, start) for first, size, owner, start in piece]
                base += sum(entry[1] for entry in piece)
            layout.append((dc, tuple(entries)))
    return tuple(layout)


def first_step(own):
    return swap_z(own), send_x(own, 1), send_x(own, -1)


def second_step(z1, up1, down1):
    h = z1.shape[0] // 2
    z2 = swap_z(jnp.concatenate([up1[h:], down1[h:]]))
    up2 = send_x(jnp.concatenate([up1[:h], z1[:h]]), 1)
    down2 = send_x(jnp.concatenate([down1[h:], z1[:h]]), -1)
    return z2, up2, down2


def third_step(z2, up2, down2):
    h, t = z2.shape[0] // 2, third_rows(z2.shape[0])
    down3 = jnp.concatenate([down2[h + t :], z2[h : 2 * t]])
    return swap_z(down2[2 * t - h : h]), send_x(up2[h : h + t], 1), send_x(down3, -1)


def with_core(pieces):
    return list(pieces) + [swap_core(piece) for piece in pieces]


def sum_cores(parts, kc):
    count = len(parts) // 2
    sent, got = list(parts[count:]), []
    for number in range(count):
        got.append(swap_core(sent[number]))
        if number + 1 < count:
            got[number], sent[number + 1] = after(got[number], sent[number + 1])
    steps = [mine + other for mine, other in zip(parts[:count], got)]
    pieces, sizes = [], [sum(entry[1] for entry in piece) for piece in shard_pieces(kc)]
    for step, numbers in zip(steps, ((7, 8, 9), (4, 5, 6), (0, 1, 2, 3))):
        base, cut = 0, []
        for number in numbers:
            cut.append(step[base : base + sizes[number]])
            base += sizes[number]
        pieces = cut + pieces
    return pieces


def third_back(z3, up3, down3):
    return swap_z(z3), send_x(up3, -1), send_x(down3, 1)


def second_back(z2, up2, down2, z3, up3, down3):
    h, t = z2.shape[0] // 2, third_rows(z2.shape[0])
    z2 = jnp.concatenate([z2[:h], z2[h : 2 * t] + down3[h - t :], z2[2 * t :]])
    up2 = jnp.concatenate([up2[:h], up2[h : h + t] + up3, up2[h + t :]])
    down2 = jnp.concatenate(
        [
            down2[: 2 * t - h],
            down2[2 * t - h : h] + z3,
            down2[h : h + t],
            down2[h + t :] + down3[: h - t],
        ]
    )
    return swap_z(z2), send_x(up2, -1), send_x(down2, 1)


def first_back(z1, up1, down1, z2, up2, down2):
    h = z2.shape[0] // 2
    z1 = swap_z(jnp.concatenate([z1[:h] + up2[h:] + down2[h:], z1[h:]]))
    up1 = send_x(up1 + jnp.concatenate([up2[:h], z2[:h]]), -1)
    down1 = send_x(jnp.concatenate([down1[:h], down1[h:] + down2[:h] + z2[h:]]), 1)
    return z1, up1, down1


def sum_rays(parts, far):
    first, near = parts[:NY], parts[NY] + far
    got = [col_shift(first[dy], 0, -dy) for dy in (1, 3, 2)]
    mine = first[0] + got[0] + got[1] + got[2]
    got = [col_shift(near[dy], 0, -dy) for dy in (1, 3, 2)]
    rest = near[0] + got[0] + got[1] + got[2]
    return mine[0] + col_shift(mine[1], 1, 0), rest


def spread_y(pair):
    return [pair] + [col_shift(pair, 0, dy) for dy in (1, 2, 3)]


def pad_row(row):
    return jnp.pad(row, (0, BS - row.shape[0]))[None]


def per_device(solution, residual, direction, gradient, blocks, block_rows, block_cols, counts):
    tile_blocks = blocks[0]
    width = direction.shape[1]
    kc = width
    sol, res, dirn, grad = solution.T, residual.T, direction.T, gradient.T
    row_index, col_index = lax.axis_index("row"), lax.axis_index("col")
    head = [
        counts[0, 0],
        row_index // 4,
        (row_index // 2) % 2,
        row_index % 2,
        col_index // 4,
        col_index % 4,
    ]
    head = jnp.stack(head + [jnp.int32(0)] * (HEAD - len(head))).astype(jnp.int32)
    lists = sorted_slots(block_rows[0], block_cols[0], head[0], head[1], head[2], head[3])
    meta = jnp.concatenate([head, lists])

    own = dirn
    turned = turn_blocks(tile_blocks)
    first = first_step(own)
    own_other = swap_core(own)
    ride, own_other = after(res, own_other)
    ride1, ride3 = col_shift(ride, 0, 1), col_shift(ride, 0, 3)
    first, meta, ride1, ride3 = after(first, meta, ride1, ride3)
    z1_other = swap_core(first[0])
    second = second_step(*first)
    ride, z1_other = after(ride, z1_other)
    ride2 = col_shift(ride, 0, 2)
    second, ride2, turned = after(second, ride2, turned)
    third = third_step(*second)
    others = [swap_core(piece) for piece in (*first[1:], *second)]
    rides = jnp.stack([res, ride1, ride2, ride3])
    rides, third_x = after(rides, third[1:])
    third = (third[0], *third_x)
    rides_z = col_shift(rides, 1, 0)
    others += [swap_core(piece) for piece in third]
    pieces = [own, *first, *second, *third, own_other, z1_other, *others]
    parts = forward(turned, meta, both_cores(kc), pieces, kc, (7, 14, 16))

    far = col_shift(parts[NY + 1], 1, 0)
    far, rides_z = after(far, rides_z)
    rides = [jnp.stack([rides[dy], rides_z[dy]]) for dy in range(NY)]
    image = jnp.concatenate(sum_rays(parts, far))
    norms = jnp.concatenate([jnp.sum(grad * grad, axis=1), jnp.sum(image * image, axis=1)])
    pair = jnp.stack([image, col_shift(image, 1, 0)])
    norms, pair = after(norms, pair)
    image_tile = spread_y(pair)
    norms = sum_over(norms[None], ("row", "col"))[0]
    gamma = norms[:width]
    alpha = (gamma / (norms[width:] + EPS))[:, None]
    back = backward(tile_blocks, meta, alpha, rides, image_tile, by_step(kc), kc, (4, 8, 12, 16))
    own_back, z1, up1, down1, z2, up2, down2, z3, up3, down3 = sum_cores(back, kc)
    third = third_back(z3, up3, down3)
    z2, third = after(z2, third)
    second = second_back(z2, up2, down2, *third)
    z1, up1, down1 = first_back(z1, up1, down1, *second)
    new_gradient = own_back + z1 + up1 + down1
    new_norms = jnp.sum(new_gradient * new_gradient, axis=1)
    new_norms = sum_over(pad_row(new_norms), ("row", "col"))[0, :width]
    beta = (new_norms / gamma)[:, None]
    return (sol + alpha * dirn).T, (res - alpha * image).T, (new_gradient + beta * dirn).T


def solution(mesh):
    placed = (
        P(("col", "row"), None),
        P(("row", "col"), None),
        P(("col", "row"), None),
        P(("col", "row"), None),
        P("row", "col", None, None),
        P("row", "col"),
        P("row", "col"),
        P("row", "col"),
    )
    return jax.shard_map(
        per_device,
        mesh=mesh,
        in_specs=placed,
        out_specs=(P(("col", "row"), None), P(("row", "col"), None), P(("col", "row"), None)),
        check_vma=False,
    )
```

```python
import functools

import jax
import jax.numpy as jnp
from jax import lax
from jax.experimental import pallas as pl
from jax.experimental.pallas import tpu as pltpu
from jax.sharding import PartitionSpec as P

EPS = 1e-06
BS = 128
GROUP = 16
HEAD = 8
NEAR = ((0, 0), (0, 1), (3, 0), (1, 0), (2, 0), (3, 1), (1, 1))
SEQUENCE = tuple((dx, dz, dc) for dc in (0, 1) for dx, dz in NEAR) + ((2, 1, 0), (2, 1, 1))
YROWS = 40
BUFFERS = 6
VMEM_BYTES = 32 * 1024 * 1024

NX, NZ, NCORE = 4, 2, 2
NZH, NY = 2, 4


def row_of(x, z, c):
    return (x % NX) * 4 + (z % NZ) * 2 + c % NCORE


def col_of(z, y):
    return (z % NZH) * 4 + y % NY


def row_shift(value, dx, dz, dc):
    pairs = [
        (row_of(x + dx, z + dz, c + dc), row_of(x, z, c))
        for x in range(NX)
        for z in range(NZ)
        for c in range(NCORE)
    ]
    return lax.ppermute(value, "row", pairs)


def col_shift(value, dz, dy):
    pairs = [(col_of(z + dz, y + dy), col_of(z, y)) for z in range(NZH) for y in range(NY)]
    return lax.ppermute(value, "col", pairs)


def sum_over(row, axes):
    count = lax.axis_size(axes)
    sent = jnp.broadcast_to(row[None], (count, 1, row.shape[1]))
    return jnp.sum(lax.all_to_all(sent, axes, 0, 0, tiled=True), axis=0)


def split(value):
    high = value.astype(jnp.bfloat16)
    low = (value - high.astype(jnp.float32)).astype(jnp.bfloat16)
    return high, low


def doubled(value):
    high, low = split(value)
    return jnp.concatenate(
        [jnp.concatenate([high, high], axis=1), jnp.concatenate([low, low], axis=1)], axis=0
    )


def fetch(blocks, held, sems, meta_ref, group):
    buffer = group % BUFFERS
    for inner in range(GROUP):
        slot = meta_ref[HEAD + group * GROUP + inner]
        pltpu.make_async_copy(blocks.at[slot], held.at[buffer, inner], sems.at[buffer]).start()


def run_groups(blocks, held, sems, meta_ref, start, stop, total, work):
    def one(group, _):
        buffer = group % BUFFERS
        pltpu.make_async_copy(blocks.at[pl.ds(0, GROUP)], held.at[buffer], sems.at[buffer]).wait()
        work(group, buffer)

        @pl.when(group + BUFFERS < total)
        def _():
            fetch(blocks, held, sems, meta_ref, group + BUFFERS)

        return 0

    lax.fori_loop(start, stop, one, 0)


def fetch_first(blocks, held, sems, meta_ref, total):
    def one(group, _):
        fetch(blocks, held, sems, meta_ref, group)
        return 0

    lax.fori_loop(0, jnp.minimum(total, BUFFERS), one, 0)


def ends_of(meta_ref, slots, position):
    return meta_ref[HEAD + 3 * (slots + GROUP) + position]


def owner_of(meta_ref, place):
    dx, dz, dc = place
    x, z, c = meta_ref[1], meta_ref[2], meta_ref[3]
    return ((x + dx) % NX) * 4 + ((z + dz) % NZ) * 2 + (c + dc) % NCORE


def turn_kernel(blocks_ref, out_ref, taken, turned, in_sems, out_sems):
    depth = taken.shape[0]
    total = blocks_ref.shape[0] // GROUP

    def take(chunk):
        span = pl.ds(chunk * GROUP, GROUP)
        buffer = chunk % depth
        return pltpu.make_async_copy(blocks_ref.at[span], taken.at[buffer], in_sems.at[buffer])

    def give(chunk):
        span = pl.ds(chunk * GROUP, GROUP)
        buffer = chunk % depth
        return pltpu.make_async_copy(turned.at[buffer], out_ref.at[span], out_sems.at[buffer])

    for chunk in range(depth):
        take(chunk).start()

    def work(chunk, _):
        buffer = chunk % depth
        take(chunk).wait()

        @pl.when(chunk >= depth)
        def _():
            give(chunk - depth).wait()

        for inner in range(GROUP):
            high, low = split(taken[buffer, inner].T)
            turned[buffer, inner, :BS] = high
            turned[buffer, inner, BS:] = low
        give(chunk).start()

        @pl.when(chunk + depth < total)
        def _():
            take(chunk + depth).start()

        return 0

    lax.fori_loop(0, total, work, 0)
    for chunk in range(total - depth, total):
        give(chunk).wait()


def turn_blocks(blocks):
    depth = 4
    shape = (blocks.shape[0], 2 * BS, BS)
    return pl.pallas_call(
        turn_kernel,
        in_specs=[pl.BlockSpec(memory_space=pltpu.HBM)],
        out_specs=pl.BlockSpec(memory_space=pltpu.HBM),
        scratch_shapes=[
            pltpu.VMEM((depth, GROUP, BS, BS), jnp.float32),
            pltpu.VMEM((depth, GROUP, 2 * BS, BS), jnp.bfloat16),
            pltpu.SemaphoreType.DMA((depth,)),
            pltpu.SemaphoreType.DMA((depth,)),
        ],
        out_shape=jax.ShapeDtypeStruct(shape, jnp.bfloat16),
        compiler_params=pltpu.CompilerParams(vmem_limit_bytes=16 * 1024 * 1024),
        cost_estimate=pl.CostEstimate(
            flops=0, bytes_accessed=8 * blocks.size, transcendentals=0
        ),
    )(blocks)


def forward_kernel(kc, slots, stages, places, meta_ref, blocks_ref, *refs):
    pieces = refs[: len(places)]
    outs = refs[len(places) : len(places) + NY + NZH]
    acc, panel, held, sems, block_sems = refs[len(places) + NY + NZH :]
    last = ends_of(meta_ref, slots, len(SEQUENCE) - 1)
    total = (last + GROUP - 1) // GROUP

    copies = []
    for number, (dc, entries) in enumerate(places):
        for source, size, (dx, dz), start in entries:
            position = SEQUENCE.index((dx, dz, dc))
            copy = pltpu.make_async_copy(
                pieces[number].at[pl.ds(source, size)],
                panel.at[position, pl.ds(start, size), :],
                sems.at[len(copies)],
            )
            copies.append((position, copy))
    for position, copy in copies:
        if position < stages[0]:
            copy.start()
    fetch_first(blocks_ref, held, block_sems, meta_ref, total)
    for position, copy in copies:
        if position >= stages[0]:
            copy.start()
    acc[...] = jnp.zeros_like(acc)

    def work(group, buffer):
        for inner in range(GROUP):
            slot = group * GROUP + inner
            place = meta_ref[HEAD + 2 * (slots + GROUP) + slot]
            offset = pl.multiple_of((place % 32) * BS, BS)
            both = jnp.dot(
                doubled(panel[place // 32, :, pl.ds(offset, BS)]),
                held[buffer, inner],
                preferred_element_type=jnp.float32,
            )
            live = jnp.where(slot < last, 1.0, 0.0)
            acc[meta_ref[HEAD + slots + GROUP + slot]] += (both[:kc] + both[kc:]) * live

    done, waited = 0, 0
    for stage in stages:
        for position, copy in copies:
            if waited <= position < stage:
                copy.wait()
        waited = stage
        stop = total if stage == stages[-1] else ends_of(meta_ref, slots, stage - 1) // GROUP
        run_groups(blocks_ref, held, block_sems, meta_ref, done, stop, total, work)
        done = stop

    zh, y = meta_ref[4], meta_ref[5]
    per = acc.shape[0] // (NZH * NY)
    for dy in range(NY):
        for dz in range(NZH):
            piece = ((zh + dz) % NZH) * 4 + (y + dy) % NY
            for t in range(per):
                both = acc[piece * per + t]
                outs[dy][dz, :, t * BS : (t + 1) * BS] = both[:YROWS]
                outs[NY + dz][dy, :, t * BS : (t + 1) * BS] = both[YROWS:]


def backward_kernel(kc, slots, stages, layout, meta_ref, blocks_ref, alpha_ref, *refs):
    res = refs[:NY]
    img = refs[NY : 2 * NY]
    outs = refs[2 * NY : 2 * NY + len(layout)]
    source, acc, held, sems, block_sems = refs[2 * NY + len(layout) :]
    last = ends_of(meta_ref, slots, len(SEQUENCE) - 1)
    total = (last + GROUP - 1) // GROUP
    fetch_first(blocks_ref, held, block_sems, meta_ref, total)

    zh, y = meta_ref[4], meta_ref[5]
    per = source.shape[0] // (NZH * NY)
    alpha = alpha_ref[...]
    for dy in range(NY):
        for dz in range(NZH):
            piece = ((zh + dz) % NZH) * 4 + (y + dy) % NY
            for t in range(per):
                span = slice(t * BS, (t + 1) * BS)
                value = res[dy][dz, :, span] - alpha * img[dy][dz, :, span]
                source[piece * per + t] = doubled(value)

    def clear(i, _):
        acc[i] = jnp.zeros(acc.shape[1:], jnp.float32)
        return 0

    lax.fori_loop(0, acc.shape[0], clear, 0)

    def work(group, buffer):
        for inner in range(GROUP):
            slot = group * GROUP + inner
            left = source[meta_ref[HEAD + slots + GROUP + slot]]
            high, low = split(held[buffer, inner])
            right = jnp.concatenate([high, low], axis=0)
            both = lax.dot_general(
                left, right, (((1,), (0,)), ((), ())), preferred_element_type=jnp.float32
            )
            live = jnp.where(slot < last, 1.0, 0.0)
            place = meta_ref[HEAD + 2 * (slots + GROUP) + slot]
            offset = pl.multiple_of((place % 32) * BS, BS)
            acc[place // 32, :, pl.ds(offset, BS)] += (both[:kc] + both[kc:]) * live

    copies = []
    for number, (dc, entries) in enumerate(layout):
        for target, size, (dx, dz), start in entries:
            position = SEQUENCE.index((dx, dz, dc))
            copy = pltpu.make_async_copy(
                acc.at[position, pl.ds(start, size), :],
                outs[number].at[pl.ds(target, size)],
                sems.at[len(copies)],
            )
            copies.append((position, copy))
    done, sent = 0, 0
    for stage in stages:
        stop = (ends_of(meta_ref, slots, stage - 1) + GROUP - 1) // GROUP
        run_groups(blocks_ref, held, block_sems, meta_ref, done, stop, total, work)
        done = stop
        for position, copy in copies:
            if sent <= position < stage:
                copy.start()
        sent = stage
    for _, copy in copies:
        copy.wait()


def cost(kc, slots, shards):
    return pl.CostEstimate(
        flops=6 * slots * BS * BS * kc,
        bytes_accessed=4 * (slots * BS * BS + 2 * shards * kc * 4096),
        transcendentals=0,
    )


def forward(blocks, meta, places, pieces, kc, stages):
    slots = blocks.shape[0]
    smem, vmem = pl.BlockSpec(memory_space=pltpu.SMEM), pl.BlockSpec(memory_space=pltpu.VMEM)
    any_spec = pl.BlockSpec(memory_space=pl.ANY)
    out_shape = [jax.ShapeDtypeStruct((NZH, YROWS, 6 * BS), jnp.float32)] * NY
    out_shape += [jax.ShapeDtypeStruct((NY, kc - YROWS, 6 * BS), jnp.float32)] * NZH
    return pl.pallas_call(
        functools.partial(forward_kernel, kc, slots, stages, places),
        in_specs=[smem, pl.BlockSpec(memory_space=pltpu.HBM)] + [any_spec] * len(pieces),
        out_specs=[vmem] * len(out_shape),
        scratch_shapes=[
            pltpu.VMEM((48, kc, BS), jnp.float32),
            pltpu.VMEM((16, kc, 4096), jnp.float32),
            pltpu.VMEM((BUFFERS, GROUP, 2 * BS, BS), jnp.bfloat16),
            pltpu.SemaphoreType.DMA((sum(len(entries) for _, entries in places),)),
            pltpu.SemaphoreType.DMA((BUFFERS,)),
        ],
        out_shape=out_shape,
        compiler_params=pltpu.CompilerParams(vmem_limit_bytes=VMEM_BYTES),
        cost_estimate=cost(kc, slots, len(SEQUENCE)),
    )(meta, blocks, *pieces)


def backward(blocks, meta, alpha, res, img, layout, kc, stages):
    slots = blocks.shape[0]
    smem, vmem = pl.BlockSpec(memory_space=pltpu.SMEM), pl.BlockSpec(memory_space=pltpu.VMEM)
    any_spec = pl.BlockSpec(memory_space=pl.ANY)
    shapes = [(sum(entry[1] for entry in entries), 4096) for _, entries in layout]
    return pl.pallas_call(
        functools.partial(backward_kernel, kc, slots, stages, layout),
        in_specs=[smem] + [any_spec] + [vmem] * (1 + 2 * NY),
        out_specs=[any_spec] * len(layout),
        scratch_shapes=[
            pltpu.VMEM((48, 2 * kc, 2 * BS), jnp.bfloat16),
            pltpu.VMEM((16, kc, 4096), jnp.float32),
            pltpu.VMEM((BUFFERS, GROUP, BS, BS), jnp.float32),
            pltpu.SemaphoreType.DMA((sum(len(entries) for _, entries in layout),)),
            pltpu.SemaphoreType.DMA((BUFFERS,)),
        ],
        out_shape=[jax.ShapeDtypeStruct(shape, jnp.float32) for shape in shapes],
        compiler_params=pltpu.CompilerParams(vmem_limit_bytes=VMEM_BYTES),
        cost_estimate=cost(kc, slots, len(SEQUENCE)),
    )(meta, blocks, alpha, *res, *img)


def sorted_slots(rows, cols, count, x, z, c):
    slots = rows.shape[0]
    number = jnp.arange(slots, dtype=jnp.int32)
    owner = cols // 32
    code = ((owner // 4 - x) % NX) * 4 + ((owner // 2 - z) % NZ) * 2 + (owner - c) % NCORE
    codes = jnp.array([dx * 4 + dz * 2 + dc for dx, dz, dc in SEQUENCE], jnp.int32)
    steps = jnp.arange(len(SEQUENCE), dtype=jnp.int32)
    position = jnp.sum(jnp.where(code[:, None] == codes, steps, 0), axis=1)
    live = number < count
    key = jnp.where(live, position, len(SEQUENCE)) * slots + number
    rank = jnp.sum((key[None] < key[:, None]).astype(jnp.int32), axis=1)
    where = rank[None] == number[:, None]
    place = position * 32 + cols % 32
    lists = [jnp.sum(jnp.where(where, value[None], 0), axis=1) for value in (number, rows, place)]
    ends = jnp.sum((live[None] & (position[None] <= steps[:, None])).astype(jnp.int32), axis=1)
    pad = jnp.zeros((GROUP,), jnp.int32)
    return jnp.concatenate([part for value in lists for part in (value, pad)] + [ends])


def after(*values):
    return lax.optimization_barrier(values)


def swap_core(value):
    return row_shift(value, 0, 0, 1)


def swap_z(value):
    return row_shift(value, 0, 1, 0)


def send_x(value, step):
    return row_shift(value, -step, 0, 0)


def third_rows(kc):
    return 3 * kc // 8


def shard_pieces(kc):
    h, t = kc // 2, third_rows(kc)
    return (
        ((0, kc, (0, 0), 0),),
        ((0, kc, (0, 1), 0),),
        ((0, kc, (3, 0), 0),),
        ((0, kc, (1, 0), 0),),
        ((0, h, (3, 1), h), (h, h, (1, 1), h)),
        ((0, h, (2, 0), 0), (h, h, (3, 1), 0)),
        ((0, h, (2, 0), h), (h, h, (1, 1), 0)),
        ((0, kc - 2 * t, (2, 1), 2 * t),),
        ((0, t, (2, 1), 0),),
        ((0, t, (2, 1), t),),
    )


def both_cores(kc):
    return tuple((dc, entries) for dc in range(NCORE) for entries in shard_pieces(kc))


def by_step(kc):
    pieces = shard_pieces(kc)
    layout = []
    for dc in range(NCORE):
        for step in (pieces[7:], pieces[4:7], pieces[:4]):
            entries, base = [], 0
            for piece in step:
                entries += [(base + first, size, owner, start) for first, size, owner, start in piece]
                base += sum(entry[1] for entry in piece)
            layout.append((dc, tuple(entries)))
    return tuple(layout)


def first_step(own):
    return swap_z(own), send_x(own, 1), send_x(own, -1)


def second_step(z1, up1, down1):
    h = z1.shape[0] // 2
    z2 = swap_z(jnp.concatenate([up1[h:], down1[h:]]))
    up2 = send_x(jnp.concatenate([up1[:h], z1[:h]]), 1)
    down2 = send_x(jnp.concatenate([down1[h:], z1[:h]]), -1)
    return z2, up2, down2


def third_step(z2, up2, down2):
    h, t = z2.shape[0] // 2, third_rows(z2.shape[0])
    down3 = jnp.concatenate([down2[h + t :], z2[h : 2 * t]])
    return swap_z(down2[2 * t - h : h]), send_x(up2[h : h + t], 1), send_x(down3, -1)


def with_core(pieces):
    return list(pieces) + [swap_core(piece) for piece in pieces]


def sum_cores(parts, kc):
    count = len(parts) // 2
    sent, got = list(parts[count:]), []
    for number in range(count):
        got.append(swap_core(sent[number]))
        if number + 1 < count:
            got[number], sent[number + 1] = after(got[number], sent[number + 1])
    steps = [mine + other for mine, other in zip(parts[:count], got)]
    pieces, sizes = [], [sum(entry[1] for entry in piece) for piece in shard_pieces(kc)]
    for step, numbers in zip(steps, ((7, 8, 9), (4, 5, 6), (0, 1, 2, 3))):
        base, cut = 0, []
        for number in numbers:
            cut.append(step[base : base + sizes[number]])
            base += sizes[number]
        pieces = cut + pieces
    return pieces


def third_back(z3, up3, down3):
    return swap_z(z3), send_x(up3, -1), send_x(down3, 1)


def second_back(z2, up2, down2, z3, up3, down3):
    h, t = z2.shape[0] // 2, third_rows(z2.shape[0])
    z2 = jnp.concatenate([z2[:h], z2[h : 2 * t] + down3[h - t :], z2[2 * t :]])
    up2 = jnp.concatenate([up2[:h], up2[h : h + t] + up3, up2[h + t :]])
    down2 = jnp.concatenate(
        [
            down2[: 2 * t - h],
            down2[2 * t - h : h] + z3,
            down2[h : h + t],
            down2[h + t :] + down3[: h - t],
        ]
    )
    return swap_z(z2), send_x(up2, -1), send_x(down2, 1)


def first_back(z1, up1, down1, z2, up2, down2):
    h = z2.shape[0] // 2
    z1 = swap_z(jnp.concatenate([z1[:h] + up2[h:] + down2[h:], z1[h:]]))
    up1 = send_x(up1 + jnp.concatenate([up2[:h], z2[:h]]), -1)
    down1 = send_x(jnp.concatenate([down1[:h], down1[h:] + down2[:h] + z2[h:]]), 1)
    return z1, up1, down1


def sum_rays(parts, far):
    first, near = parts[:NY], parts[NY] + far
    got = [col_shift(first[dy], 0, -dy) for dy in (1, 3, 2)]
    mine = first[0] + got[0] + got[1] + got[2]
    got = [col_shift(near[dy], 0, -dy) for dy in (1, 3, 2)]
    rest = near[0] + got[0] + got[1] + got[2]
    return mine[0] + col_shift(mine[1], 1, 0), rest


def spread_y(pair):
    return [pair] + [col_shift(pair, 0, dy) for dy in (1, 2, 3)]


def pad_row(row):
    return jnp.pad(row, (0, BS - row.shape[0]))[None]


def per_device(solution, residual, direction, gradient, blocks, block_rows, block_cols, counts):
    tile_blocks = blocks[0]
    width = direction.shape[1]
    kc = width
    sol, res, dirn, grad = solution.T, residual.T, direction.T, gradient.T
    row_index, col_index = lax.axis_index("row"), lax.axis_index("col")
    head = [
        counts[0, 0],
        row_index // 4,
        (row_index // 2) % 2,
        row_index % 2,
        col_index // 4,
        col_index % 4,
    ]
    head = jnp.stack(head + [jnp.int32(0)] * (HEAD - len(head))).astype(jnp.int32)
    lists = sorted_slots(block_rows[0], block_cols[0], head[0], head[1], head[2], head[3])
    meta = jnp.concatenate([head, lists])

    own = dirn
    turned = turn_blocks(tile_blocks)
    first = first_step(own)
    own_other = swap_core(own)
    ride, own_other = after(res, own_other)
    ride1, ride3 = col_shift(ride, 0, 1), col_shift(ride, 0, 3)
    first, meta, ride1, ride3 = after(first, meta, ride1, ride3)
    z1_other = swap_core(first[0])
    second = second_step(*first)
    ride, z1_other = after(ride, z1_other)
    ride2 = col_shift(ride, 0, 2)
    second, ride2, turned = after(second, ride2, turned)
    third = third_step(*second)
    others = [swap_core(piece) for piece in (*first[1:], *second)]
    rides = jnp.stack([res, ride1, ride2, ride3])
    rides, third_x = after(rides, third[1:])
    third = (third[0], *third_x)
    rides_z = col_shift(rides, 1, 0)
    others += [swap_core(piece) for piece in third]
    pieces = [own, *first, *second, *third, own_other, z1_other, *others]
    parts = forward(turned, meta, both_cores(kc), pieces, kc, (7, 14, 16))

    far = col_shift(parts[NY + 1], 1, 0)
    far, rides_z = after(far, rides_z)
    rides = [jnp.stack([rides[dy], rides_z[dy]]) for dy in range(NY)]
    image = jnp.concatenate(sum_rays(parts, far))
    norms = jnp.concatenate([jnp.sum(grad * grad, axis=1), jnp.sum(image * image, axis=1)])
    pair = jnp.stack([image, col_shift(image, 1, 0)])
    norms, pair = after(norms, pair)
    image_tile = spread_y(pair)
    norms = sum_over(norms[None], ("row", "col"))[0]
    gamma = norms[:width]
    alpha = (gamma / (norms[width:] + EPS))[:, None]
    back = backward(tile_blocks, meta, alpha, rides, image_tile, by_step(kc), kc, (4, 8, 12, 16))
    own_back, z1, up1, down1, z2, up2, down2, z3, up3, down3 = sum_cores(back, kc)
    third = third_back(z3, up3, down3)
    z2, third = after(z2, third)
    second = second_back(z2, up2, down2, *third)
    z1, up1, down1 = first_back(z1, up1, down1, *second)
    new_gradient = own_back + z1 + up1 + down1
    new_norms = jnp.sum(new_gradient * new_gradient, axis=1)
    new_norms = sum_over(pad_row(new_norms), ("row", "col"))[0, :width]
    beta = (new_norms / gamma)[:, None]
    return (sol + alpha * dirn).T, (res - alpha * image).T, (new_gradient + beta * dirn).T


def solution(mesh):
    placed = (
        P(("col", "row"), None),
        P(("row", "col"), None),
        P(("col", "row"), None),
        P(("col", "row"), None),
        P("row", "col", None, None),
        P("row", "col"),
        P("row", "col"),
        P("row", "col"),
    )
    return jax.shard_map(
        per_device,
        mesh=mesh,
        in_specs=placed,
        out_specs=(P(("col", "row"), None), P(("row", "col"), None), P(("col", "row"), None)),
        check_vma=False,
    )
```
